512 devices in a mesh: ctx: 64 (over z, x, core), head: 8 (over y).
Axes of the slice: x: 4, y: 8, z: 8, core: 2. Of those that a mesh axis runs over, the one named last changes fastest.
Arguments:
- queries: bfloat16 [8192, 8192], P('ctx', 'head'), may hold values from -6 to 6
- keys: bfloat16 [8192, 1024], P(('ctx', 'head')), may hold values from -6 to 6
- values: bfloat16 [8192, 1024], P(('ctx', 'head')), may hold values from -6 to 6
- output_gradient: bfloat16 [8192, 8192], P('ctx', 'head'), may hold values from -6 to 6
- doc_lengths: int32 [128], replicated, may hold values from 1 to 640, 8192 in all
Outputs:
- attended: bfloat16 [8192, 8192], P('ctx', 'head')
- grad_queries: bfloat16 [8192, 8192], P('ctx', 'head')
- key_gradient: bfloat16 [8192, 1024], P(('ctx', 'head'))
- value_gradient: bfloat16 [8192, 1024], P(('ctx', 'head'))
The draws below stay inside these ranges and needn't reach their ends.
Inputs may be any that keep to these rules, and one draw needn't show every extreme that they name: `doc_lengths`: the lengths sum to 8192; the longest is exactly 640.
All inputs are finite; a program needn't handle non-finite values.
Results may differ from the reference program's by a relative error of at most 0.03.
Values may be sent and summed in bfloat16 or wider, within the bound.
A program may use at most 64 MiB of HBM per device.

```python
import math
import jax
import jax.numpy as jnp
import numpy as np
from jax import lax

QUERY_HEADS = 64
KEY_VALUE_HEADS = 8
HEAD_SIZE = 128
TOK_DEV = 128
SPAN = 5
WINDOW_TOKENS = 8192
DOC_MOST = 640
NDOCS = 128


def draw_queries(key, part):
    key = jax.random.fold_in(key, 3)
    head_group = QUERY_HEADS // KEY_VALUE_HEADS
    drawn_result = jnp.clip(jax.random.normal(key, (WINDOW_TOKENS, KEY_VALUE_HEADS, head_group, HEAD_SIZE), jnp.float32), -6.0, 6.0)
    return drawn_result.reshape(WINDOW_TOKENS, QUERY_HEADS * HEAD_SIZE).astype(jnp.bfloat16)


def draw_keys(key, part):
    key = jax.random.fold_in(key, 5)
    drawn_result = jnp.clip(jax.random.normal(key, (WINDOW_TOKENS, KEY_VALUE_HEADS, HEAD_SIZE), jnp.float32), -6.0, 6.0)
    return drawn_result.reshape(WINDOW_TOKENS, KEY_VALUE_HEADS * HEAD_SIZE).astype(jnp.bfloat16)


def shard_levels(rng, extent, pieces, smallest, largest):
    def one(dim, blocks):
        steps = jax.random.uniform(jax.random.fold_in(jax.random.fold_in(rng, 6), dim), (blocks,), jnp.float32, smallest / len(pieces), largest / len(pieces))
        return jnp.repeat(jnp.exp(steps), extent[dim] // blocks).reshape((-1,) + (1,) * (len(extent) - dim - 1))

    level = one(*pieces[0])
    for cut in pieces[1:]:
        level = level * one(*cut)
    return level


def split_up(count, total, most, lean):
    loads = [(1 << 20) // math.isqrt(standing ** lean) + 1 for standing in range(2, count + 1)]
    spare, given = total - most - (count - 1), [1] * (count - 1)
    while spare > 0:
        free = [i for i in range(count - 1) if given[i] < most]
        whole, budget = sum([loads[i] for i in free]), spare
        for i in free:
            addition = min(most - given[i], max(1, budget * loads[i] // whole), spare)
            given[i] = given[i] + addition
            spare = spare - addition
    return np.array([most] + given)


def ragged(stream_key, count, total, reach, slope):
    if count == 2:
        one = jax.random.randint(stream_key, (), max(1, total - reach), min(reach, total - 1) + 1)
        return jnp.stack([one, total - one])
    tallies = jnp.asarray(split_up(count, total, reach, slope), jnp.int32)
    twos = (count - 1) // 2
    donor, taker = tallies[1:1 + 2 * twos:2], tallies[2:2 + 2 * twos:2]
    margin = jnp.minimum(donor - 1, reach - taker)
    shifted = jax.random.randint(jax.random.fold_in(stream_key, 1), (twos,), 0, 1 << 20) % (margin + 1)
    tallies = tallies.at[1:1 + 2 * twos:2].set(donor - shifted).at[2:2 + 2 * twos:2].set(taker + shifted)
    return tallies[jax.random.permutation(jax.random.fold_in(stream_key, 2), count)]


def normal_values(rng, shape, scale, most, cuts=(), held_as=jnp.bfloat16):
    factor_of = shard_levels(rng, shape, cuts, -0.22, 0.18) if cuts else 1.0
    entries = jax.random.normal(rng, shape, jnp.float32) * scale * factor_of
    return jnp.minimum(jnp.maximum(entries, -most), most).astype(held_as)


def setup_inputs(seed: int = 0) -> dict:
    splits = jax.random.split(jax.random.key(seed), 6)
    queries = draw_queries(jax.random.fold_in(splits[5], 71), 0)
    keys = draw_keys(jax.random.fold_in(splits[5], 71), 0)
    values = normal_values(splits[2], (WINDOW_TOKENS, KEY_VALUE_HEADS * HEAD_SIZE), 1.0, 6.0, ((0, 512),))
    output_gradient = normal_values(splits[3], (WINDOW_TOKENS, QUERY_HEADS * HEAD_SIZE), 1.0, 6.0, ((0, 64), (1, 8)))
    doc_lengths = ragged(splits[4], NDOCS, WINDOW_TOKENS, DOC_MOST, 2).astype(jnp.int32)
    return {"queries": queries, "keys": keys, "values": values, "output_gradient": output_gradient, "doc_lengths": doc_lengths}


def document_ids(doc_lengths, positions):
    ends = jnp.cumsum(doc_lengths)
    return jnp.sum((positions[:, None] >= ends[None, :]).astype(jnp.int32), axis=1).astype(jnp.int32)


def reference(queries, keys, values, output_gradient, doc_lengths):
    scale = HEAD_SIZE ** -0.5
    head_group = QUERY_HEADS // KEY_VALUE_HEADS
    reach_length = SPAN * TOK_DEV
    width = reach_length + TOK_DEV
    blocks = WINDOW_TOKENS // TOK_DEV
    positions = jnp.arange(WINDOW_TOKENS, dtype=jnp.int32)
    query_docs = document_ids(doc_lengths, positions)
    key_docs = jnp.concatenate([jnp.full((reach_length,), -1, jnp.int32), query_docs])
    key_pos = (jnp.arange(WINDOW_TOKENS + reach_length, dtype=jnp.int32) - reach_length).astype(jnp.int32)
    query_groups = queries.reshape(WINDOW_TOKENS, KEY_VALUE_HEADS, head_group, HEAD_SIZE).transpose(1, 0, 2, 3)
    gradient_groups = output_gradient.reshape(WINDOW_TOKENS, KEY_VALUE_HEADS, head_group, HEAD_SIZE).transpose(1, 0, 2, 3)
    padding_amount = jnp.zeros((KEY_VALUE_HEADS, reach_length, HEAD_SIZE), keys.dtype)
    key_groups = jnp.concatenate([padding_amount, keys.reshape(WINDOW_TOKENS, KEY_VALUE_HEADS, HEAD_SIZE).transpose(1, 0, 2)], axis=1)
    value_groups = jnp.concatenate([padding_amount, values.reshape(WINDOW_TOKENS, KEY_VALUE_HEADS, HEAD_SIZE).transpose(1, 0, 2)], axis=1)

    def one_group(operands):
        q_all, g_all, k_all, v_all = operands

        def step(carry, block):
            dk_acc, dv_acc = carry
            start = (block * TOK_DEV).astype(jnp.int32)
            q_blk = lax.dynamic_slice_in_dim(q_all, start, TOK_DEV, 0).astype(jnp.float32)
            g_blk = lax.dynamic_slice_in_dim(g_all, start, TOK_DEV, 0).astype(jnp.float32)
            k_blk = lax.dynamic_slice_in_dim(k_all, start, width, 0).astype(jnp.float32)
            v_blk = lax.dynamic_slice_in_dim(v_all, start, width, 0).astype(jnp.float32)
            q_doc = lax.dynamic_slice_in_dim(query_docs, start, TOK_DEV, 0)
            q_pos = lax.dynamic_slice_in_dim(positions, start, TOK_DEV, 0)
            k_doc = lax.dynamic_slice_in_dim(key_docs, start, width, 0)
            k_pos = lax.dynamic_slice_in_dim(key_pos, start, width, 0)
            visible = (q_doc[:, None] == k_doc[None, :]) & (k_pos[None, :] <= q_pos[:, None])
            scores = jnp.einsum('rhd,kd->hrk', q_blk, k_blk) * scale
            scores = jnp.where(visible[None], scores, -1e30)
            top = jnp.max(scores, axis=2, keepdims=True)
            lse = top + jnp.log(jnp.sum(jnp.exp(scores - top), axis=2, keepdims=True))
            probs = jnp.exp(scores - lse).astype(jnp.bfloat16).astype(jnp.float32)
            out = jnp.einsum('hrk,kd->rhd', probs, v_blk).astype(jnp.bfloat16)
            delta = jnp.sum(g_blk * out.astype(jnp.float32), axis=2).T
            dprobs = jnp.einsum('rhd,kd->hrk', g_blk, v_blk)
            dscores = (probs * (dprobs - delta[:, :, None]) * scale).astype(jnp.bfloat16).astype(jnp.float32)
            dq = jnp.einsum('hrk,kd->rhd', dscores, k_blk).astype(jnp.bfloat16)
            dk = jnp.einsum('hrk,rhd->kd', dscores, q_blk)
            dv = jnp.einsum('hrk,rhd->kd', probs, g_blk)
            dk_acc = lax.dynamic_update_slice_in_dim(dk_acc, lax.dynamic_slice_in_dim(dk_acc, start, width, 0) + dk, start, 0)
            dv_acc = lax.dynamic_update_slice_in_dim(dv_acc, lax.dynamic_slice_in_dim(dv_acc, start, width, 0) + dv, start, 0)
            return (dk_acc, dv_acc), (out, dq)

        empty = jnp.zeros((WINDOW_TOKENS + reach_length, HEAD_SIZE), jnp.float32)
        (dk_acc, dv_acc), (outs, dqs) = lax.scan(step, (empty, empty), jnp.arange(blocks, dtype=jnp.int32))
        return (outs.reshape(WINDOW_TOKENS, head_group, HEAD_SIZE), dqs.reshape(WINDOW_TOKENS, head_group, HEAD_SIZE),
                dk_acc[reach_length:].astype(jnp.bfloat16), dv_acc[reach_length:].astype(jnp.bfloat16))

    outs, dqs, key_gradient_parts, value_gradient_parts = lax.map(one_group, (query_groups, gradient_groups, key_groups, value_groups))
    attended = outs.transpose(1, 0, 2, 3).reshape(WINDOW_TOKENS, QUERY_HEADS * HEAD_SIZE)
    grad_queries = dqs.transpose(1, 0, 2, 3).reshape(WINDOW_TOKENS, QUERY_HEADS * HEAD_SIZE)
    key_gradient = key_gradient_parts.transpose(1, 0, 2).reshape(WINDOW_TOKENS, KEY_VALUE_HEADS * HEAD_SIZE)
    value_gradient = value_gradient_parts.transpose(1, 0, 2).reshape(WINDOW_TOKENS, KEY_VALUE_HEADS * HEAD_SIZE)
    return attended, grad_queries, key_gradient, value_gradient
```

```python
import functools

import jax
import jax.numpy as jnp
from jax import lax
from jax.experimental import pallas as pl
from jax.experimental.pallas import tpu as pltpu
from jax.sharding import PartitionSpec as P

HEAD_SIZE = 128
SCALE = HEAD_SIZE ** (-0.5)
LOG2E = 1.4426950408889634
big_negative = -1e30
MESH = pl.DeviceIdType.MESH
F32 = jnp.float32
BF16 = jnp.bfloat16

OWN = 0
NEAR = 1
FAR = 2
CROSS = 3
NEAR_SIB = 4
FAR_SIB = 5
ROLES = 6


def kernel(
    n_ctx,
    n_head,
    tokens,
    heads,
    q_hbm,
    k_hbm,
    v_hbm,
    g_hbm,
    len_hbm,
    att_hbm,
    dq_hbm,
    dk_out,
    dv_out,
    k_in,
    v_in,
    lens,
    q_rows,
    g_rows,
    q_cols,
    g_cols,
    kv_stage,
    kv,
    k_cols,
    v_cols,
    probs,
    dprobs,
    dscores,
    part,
    back,
    grad_stage,
    grad_in,
    att,
    dq,
    in_sem,
    out_sem,
    y_send,
    y_recv,
    c_send,
    c_recv,
    b_send,
    b_recv,
    z_send,
    z_recv,
):
    d = HEAD_SIZE
    c = lax.axis_index("ctx")
    h = lax.axis_index("head")
    core = lax.rem(c, 2)
    piece = tokens // n_head
    width = heads * tokens

    def ctx_at(distance):
        return lax.rem(c + distance + n_ctx, n_ctx)

    sibling = c + 1 - 2 * core
    cross_to = ctx_at(1 + 4 * core)
    cross_from = ctx_at(4 * core - 5)

    loads = [
        pltpu.make_async_copy(k_hbm, k_in, in_sem.at[0]),
        pltpu.make_async_copy(v_hbm, v_in, in_sem.at[1]),
        pltpu.make_async_copy(len_hbm, lens, in_sem.at[2]),
    ]
    q_loads, g_loads = [], []
    for r in range(heads):
        cols, rows = pl.ds(r * d, d), pl.ds(r * tokens, tokens)
        q_loads.append(
            pltpu.make_async_copy(q_hbm.at[:, cols], q_rows.at[rows, :], in_sem.at[3 + r])
        )
        g_loads.append(
            pltpu.make_async_copy(g_hbm.at[:, cols], g_rows.at[rows, :], in_sem.at[3 + heads + r])
        )
    for load in loads + q_loads + g_loads:
        load.start()

    barrier = pltpu.get_barrier_semaphore()
    peers = [(c, lax.rem(h + step, n_head)) for step in range(1, n_head)]
    peers += [(ctx_at(step), h) for step in (2, -2, 4, -4)]
    peers += [(sibling, h), (jnp.where(core == 0, cross_from, cross_to), h)]
    for peer in peers:
        pl.semaphore_signal(barrier, inc=1, device_id=peer, device_id_type=MESH)

    loads[0].wait()
    loads[1].wait()
    for r in range(n_head):
        cols = slice(r * d, (r + 1) * d)
        kv_stage[r, 0] = k_in[:, cols]
        kv_stage[r, 1] = v_in[:, cols]
    kv[OWN, h] = kv_stage[h]
    pl.semaphore_wait(barrier, len(peers))

    def send(src, dst, send_sem, recv_sem, to):
        copy = pltpu.make_async_remote_copy(
            src_ref=src,
            dst_ref=dst,
            send_sem=send_sem,
            recv_sem=recv_sem,
            device_id=to,
            device_id_type=MESH,
        )
        copy.start()
        return copy

    y_copies = []
    for step in range(1, n_head):
        to = lax.rem(h + step, n_head)
        y_copies.append(
            send(kv_stage.at[to], kv.at[OWN, h], y_send.at[step], y_recv.at[step], (c, to))
        )

    loads[2].wait()
    ids_row = lax.broadcasted_iota(jnp.int32, (128, 128), 0)
    ids_col = lax.broadcasted_iota(jnp.int32, (128, 128), 1)
    ends = jnp.sum(
        jnp.where(ids_col <= ids_row, jnp.broadcast_to(lens[...], (128, 128)), 0).astype(F32),
        axis=1,
        keepdims=True,
    ).astype(jnp.int32)
    place = c * tokens + ids_col
    starts = jnp.max(jnp.where(ends <= place, ends, 0).astype(F32), axis=0, keepdims=True)
    starts = starts.astype(jnp.int32) - c * tokens
    starts = jnp.concatenate([starts] * 2, axis=1)

    for r in range(heads):
        cols, rows = slice(r * d, (r + 1) * d), slice(r * tokens, (r + 1) * tokens)
        q_loads[r].wait()
        q_cols[:, cols] = q_rows[rows, :].T
        g_loads[r].wait()
        g_cols[:, cols] = g_rows[rows, :].T

    for copy in y_copies:
        copy.wait_recv()
    c_copies = [
        send(kv.at[OWN], kv.at[FAR], c_send.at[FAR], c_recv.at[FAR], (ctx_at(4), h)),
        send(kv.at[OWN], kv.at[CROSS], c_send.at[CROSS], c_recv.at[CROSS], (cross_to, h)),
        send(kv.at[OWN], kv.at[NEAR], c_send.at[NEAR], c_recv.at[NEAR], (ctx_at(2), h)),
    ]

    chunk = 2 * tokens
    chunks = width // chunk
    key_ids = lax.broadcasted_iota(jnp.int32, (tokens, chunk), 0)
    query_ids = lax.rem(lax.broadcasted_iota(jnp.int32, (tokens, chunk), 1), tokens)
    back_by = [0, 2, 4, 5 - 4 * core, 1 + 2 * core, 3 + 2 * core]
    tops, totals, deltas = {}, {}, {}

    def forward(role):
        k_block = kv[role, :, 0].reshape(tokens, d)
        v_block = kv[role, :, 1].reshape(tokens, d)
        cols = slice(role * tokens, (role + 1) * tokens)
        k_cols[:, cols] = k_block.T
        v_cols[:, cols] = v_block.T
        visible = key_ids - back_by[role] * tokens >= starts
        if role == OWN:
            visible = visible & (key_ids <= query_ids)
        for j in range(chunks):
            qs = slice(j * chunk, (j + 1) * chunk)
            scores = jnp.dot(k_block, q_cols[:, qs], preferred_element_type=F32)
            scores = jnp.where(visible, scores, big_negative)
            top = jnp.max(scores, axis=0, keepdims=True)
            grown = jnp.exp2((scores - top) * (SCALE * LOG2E))
            dp = jnp.dot(v_block, g_cols[:, qs], preferred_element_type=F32)
            tops[role, j] = top
            totals[role, j] = jnp.sum(grown, axis=0, keepdims=True)
            deltas[role, j] = jnp.sum(grown * dp, axis=0, keepdims=True)
            probs[cols, qs] = grown.astype(BF16)
            dprobs[cols, qs] = dp

    forward(OWN)
    c_copies[2].wait_recv()
    c_copies.append(
        send(kv.at[NEAR], kv.at[NEAR_SIB], c_send.at[NEAR_SIB], c_recv.at[NEAR_SIB], (sibling, h))
    )
    c_copies[0].wait_recv()
    c_copies.append(
        send(kv.at[FAR], kv.at[FAR_SIB], c_send.at[FAR_SIB], c_recv.at[FAR_SIB], (sibling, h))
    )
    forward(NEAR)
    forward(FAR)
    c_copies[1].wait_recv()
    forward(CROSS)
    c_copies[3].wait_recv()
    forward(NEAR_SIB)
    c_copies[4].wait_recv()
    forward(FAR_SIB)

    factors, delta = {}, {}
    for j in range(chunks):
        top = functools.reduce(jnp.maximum, [tops[role, j] for role in range(ROLES)])
        lift = [jnp.exp2((tops[role, j] - top) * (SCALE * LOG2E)) for role in range(ROLES)]
        total = sum(lift[role] * totals[role, j] for role in range(ROLES))
        for role in range(ROLES):
            factors[role, j] = lift[role] / total
        delta[j] = sum(factors[role, j] * deltas[role, j] for role in range(ROLES))

    def backward(role):
        rows = slice(role * tokens, (role + 1) * tokens)
        for j in range(chunks):
            qs = slice(j * chunk, (j + 1) * chunk)
            p = probs[rows, qs].astype(F32) * factors[role, j]
            probs[rows, qs] = p.astype(BF16)
            dscores[rows, qs] = (p * (dprobs[rows, qs] - delta[j])).astype(BF16)
        dk_part = jnp.dot(dscores[rows, :], q_rows[...], preferred_element_type=F32) * SCALE
        dv_part = jnp.dot(probs[rows, :], g_rows[...], preferred_element_type=F32)
        return dk_part, dv_part

    def put(where, dk_part, dv_part):
        where[:, 0] = dk_part.astype(BF16).reshape(n_head, piece, d)
        where[:, 1] = dv_part.astype(BF16).reshape(n_head, piece, d)

    def with_back(slot, dk_part, dv_part):
        dk_part = dk_part + back[slot, :, 0].reshape(tokens, d).astype(F32)
        dv_part = dv_part + back[slot, :, 1].reshape(tokens, d).astype(F32)
        return dk_part, dv_part

    b_copies = {}

    def send_back(role, to):
        b_copies[role] = send(
            part.at[role], back.at[role], b_send.at[role], b_recv.at[role], (to, h)
        )

    put(part.at[FAR_SIB], *backward(FAR_SIB))
    send_back(FAR_SIB, sibling)
    put(part.at[NEAR_SIB], *backward(NEAR_SIB))
    send_back(NEAR_SIB, sibling)
    put(part.at[CROSS], *backward(CROSS))
    send_back(CROSS, cross_from)
    far_grads = backward(FAR)
    b_copies[FAR_SIB].wait_recv()
    put(part.at[FAR], *with_back(FAR_SIB, *far_grads))
    send_back(FAR, ctx_at(-4))
    near_grads = backward(NEAR)
    b_copies[NEAR_SIB].wait_recv()
    put(part.at[NEAR], *with_back(NEAR_SIB, *near_grads))
    send_back(NEAR, ctx_at(-2))
    own_grads = backward(OWN)

    for j in range(chunks):
        qs = slice(j * chunk, (j + 1) * chunk)
        out = jnp.dot(v_cols[...], probs[:, qs], preferred_element_type=F32).astype(BF16)
        grad = jnp.dot(k_cols[...], dscores[:, qs], preferred_element_type=F32) * SCALE
        grad = grad.astype(BF16)
        for i in range(chunk // tokens):
            r = j * (chunk // tokens) + i
            att[:, r * d : (r + 1) * d] = out[:, i * tokens : (i + 1) * tokens].T
            dq[:, r * d : (r + 1) * d] = grad[:, i * tokens : (i + 1) * tokens].T
    stores = [
        pltpu.make_async_copy(att, att_hbm, out_sem.at[0]),
        pltpu.make_async_copy(dq, dq_hbm, out_sem.at[1]),
    ]
    for store in stores:
        store.start()

    for role in (CROSS, NEAR, FAR):
        b_copies[role].wait_recv()
        own_grads = with_back(role, *own_grads)
    put(grad_stage, *own_grads)
    z_copies = []
    for step in range(1, n_head):
        to = lax.rem(h + step, n_head)
        z_copies.append(
            send(grad_stage.at[to], grad_in.at[h], z_send.at[step], z_recv.at[step], (c, to))
        )
    grad_in[h] = grad_stage[h]
    for copy in z_copies:
        copy.wait_recv()
    for r in range(n_head):
        dk_out[:, r * d : (r + 1) * d] = grad_in[r, 0]
        dv_out[:, r * d : (r + 1) * d] = grad_in[r, 1]

    for copy in y_copies + c_copies + list(b_copies.values()) + z_copies:
        copy.wait_send()
    for store in stores:
        store.wait()


def per_device(n_ctx, n_head, queries, keys, values, output_gradient, doc_lengths):
    tokens = queries.shape[0]
    piece = keys.shape[0]
    d = HEAD_SIZE
    heads = queries.shape[1] // d
    width = heads * tokens
    docs = doc_lengths.shape[0]
    any_spec = pl.BlockSpec(memory_space=pl.ANY)
    vmem_spec = pl.BlockSpec(memory_space=pltpu.VMEM)
    block = (n_head, 2, piece, d)
    dma = pltpu.SemaphoreType.DMA
    return pl.pallas_call(
        functools.partial(kernel, n_ctx, n_head, tokens, heads),
        out_shape=(
            jax.ShapeDtypeStruct(queries.shape, BF16),
            jax.ShapeDtypeStruct(queries.shape, BF16),
            jax.ShapeDtypeStruct(keys.shape, BF16),
            jax.ShapeDtypeStruct(values.shape, BF16),
        ),
        in_specs=[any_spec] * 5,
        out_specs=(any_spec, any_spec, vmem_spec, vmem_spec),
        scratch_shapes=[
            pltpu.VMEM(keys.shape, BF16),
            pltpu.VMEM(values.shape, BF16),
            pltpu.VMEM((1, docs), jnp.int32),
            pltpu.VMEM((width, d), BF16),
            pltpu.VMEM((width, d), BF16),
            pltpu.VMEM((d, width), BF16),
            pltpu.VMEM((d, width), BF16),
            pltpu.VMEM(block, BF16),
            pltpu.VMEM((ROLES, *block), BF16),
            pltpu.VMEM((d, ROLES * tokens), BF16),
            pltpu.VMEM((d, ROLES * tokens), BF16),
            pltpu.VMEM((ROLES * tokens, width), BF16),
            pltpu.VMEM((ROLES * tokens, width), F32),
            pltpu.VMEM((ROLES * tokens, width), BF16),
            pltpu.VMEM((ROLES, *block), BF16),
            pltpu.VMEM((ROLES, *block), BF16),
            pltpu.VMEM(block, BF16),
            pltpu.VMEM(block, BF16),
            pltpu.VMEM((tokens, width), BF16),
            pltpu.VMEM((tokens, width), BF16),
            dma((3 + 2 * heads,)),
            dma((2,)),
            dma((n_head,)),
            dma((n_head,)),
            dma((ROLES,)),
            dma((ROLES,)),
            dma((ROLES,)),
            dma((ROLES,)),
            dma((n_head,)),
            dma((n_head,)),
        ],
        compiler_params=pltpu.CompilerParams(
            collective_id=0, has_side_effects=True, vmem_limit_bytes=40 * 1024 * 1024
        ),
    )(queries, keys, values, output_gradient, doc_lengths.reshape(1, docs))


def solution(mesh):
    n_ctx, n_head = mesh.shape["ctx"], mesh.shape["head"]
    return jax.shard_map(
        functools.partial(per_device, n_ctx, n_head),
        mesh=mesh,
        in_specs=(
            P("ctx", "head"),
            P(("ctx", "head"), None),
            P(("ctx", "head"), None),
            P("ctx", "head"),
            P(),
        ),
        out_specs=(
            P("ctx", "head"),
            P("ctx", "head"),
            P(("ctx", "head"), None),
            P(("ctx", "head"), None),
        ),
        check_vma=False,
    )
```

```python
import functools

import jax
import jax.numpy as jnp
from jax import lax
from jax.experimental import pallas as pl
from jax.experimental.pallas import tpu as pltpu
from jax.sharding import PartitionSpec as P

HEAD_SIZE = 128
SCALE = HEAD_SIZE ** (-0.5)
LOG2E = 1.4426950408889634
big_negative = -1e30
MESH = pl.DeviceIdType.MESH
F32 = jnp.float32
BF16 = jnp.bfloat16

OWN = 0
NEAR = 1
FAR = 2
CROSS = 3
NEAR_SIB = 4
FAR_SIB = 5
ROLES = 6


class Message:
    def __init__(self, src, dst, send_sem, recv_sem, to, sends=None, receives=None):
        self.copy = pltpu.make_async_remote_copy(
            src_ref=src,
            dst_ref=dst,
            send_sem=send_sem,
            recv_sem=recv_sem,
            device_id=to,
            device_id_type=MESH,
        )
        self.sends, self.receives = sends, receives

    def start(self):
        run_if(self.sends, self.copy.start)

    def wait_recv(self):
        run_if(self.receives, self.copy.wait_recv)

    def wait_send(self):
        run_if(self.sends, self.copy.wait_send)


def run_if(condition, action):
    if condition is None:
        action()
        return

    @pl.when(condition)
    def _():
        action()


def kernel(
    n_ctx,
    n_head,
    tokens,
    heads,
    q_hbm,
    k_hbm,
    v_hbm,
    g_hbm,
    len_hbm,
    att,
    dq,
    dk_out,
    dv_out,
    k_in,
    v_in,
    lens,
    q_rows,
    g_rows,
    q_cols,
    g_cols,
    kv_stage,
    kv,
    k_cols,
    v_cols,
    probs,
    dprobs,
    dscores,
    part,
    back,
    grad_stage,
    grad_in,
    in_sem,
    y_send,
    y_recv,
    c_send,
    c_recv,
    b_send,
    b_recv,
    z_send,
    z_recv,
):
    d = HEAD_SIZE
    c = lax.axis_index("ctx")
    h = lax.axis_index("head")
    core = lax.rem(c, 2)
    piece = tokens // n_head
    width = heads * tokens

    sibling = c + 1 - 2 * core
    cross_to = c + 1 + 4 * core
    cross_from = c + 4 * core - 5
    has_from = {NEAR: c >= 2, FAR: c >= 4, CROSS: cross_from >= 0}
    has_to = {NEAR: c + 2 < n_ctx, FAR: c + 4 < n_ctx, CROSS: cross_to < n_ctx}

    loads = [
        pltpu.make_async_copy(k_hbm, k_in, in_sem.at[0]),
        pltpu.make_async_copy(v_hbm, v_in, in_sem.at[1]),
        pltpu.make_async_copy(len_hbm, lens, in_sem.at[2]),
    ]
    q_loads, g_loads = [], []
    for r in range(heads):
        cols, rows = pl.ds(r * d, d), pl.ds(r * tokens, tokens)
        q_loads.append(
            pltpu.make_async_copy(q_hbm.at[:, cols], q_rows.at[rows, :], in_sem.at[3 + r])
        )
        g_loads.append(
            pltpu.make_async_copy(g_hbm.at[:, cols], g_rows.at[rows, :], in_sem.at[3 + heads + r])
        )
    for load in loads + q_loads + g_loads:
        load.start()

    for role in (NEAR, FAR, CROSS):

        @pl.when(jnp.logical_not(has_from[role]))
        def _(role=role):
            kv[role] = jnp.zeros(kv.shape[1:], BF16)

        @pl.when(jnp.logical_not(has_to[role]))
        def _(role=role):
            back[role] = jnp.zeros(back.shape[1:], BF16)

    barrier = pltpu.get_barrier_semaphore()

    def greet(peer):
        pl.semaphore_signal(barrier, inc=1, device_id=peer, device_id_type=MESH)

    for step in range(1, n_head):
        greet((c, lax.rem(h + step, n_head)))
    greet((sibling, h))
    n_peers = n_head
    far_cross = jnp.where(core == 0, cross_from, cross_to)
    for there, peer in (
        (has_from[NEAR], c - 2),
        (has_to[NEAR], c + 2),
        (has_from[FAR], c - 4),
        (has_to[FAR], c + 4),
        ((far_cross >= 0) & (far_cross < n_ctx), far_cross),
    ):

        @pl.when(there)
        def _(peer=peer):
            greet((peer, h))

        n_peers = n_peers + jnp.where(there, 1, 0)

    loads[0].wait()
    loads[1].wait()
    for r in range(n_head):
        cols = slice(r * d, (r + 1) * d)
        kv_stage[r, 0] = k_in[:, cols]
        kv_stage[r, 1] = v_in[:, cols]
    kv[OWN, h] = kv_stage[h]
    pl.semaphore_wait(barrier, n_peers)

    def send(src, dst, send_sem, recv_sem, to, sends=None, receives=None):
        copy = Message(src, dst, send_sem, recv_sem, to, sends, receives)
        copy.start()
        return copy

    y_copies = []
    for step in range(1, n_head):
        to = lax.rem(h + step, n_head)
        y_copies.append(
            send(kv_stage.at[to], kv.at[OWN, h], y_send.at[step], y_recv.at[step], (c, to))
        )

    loads[2].wait()
    ids_row = lax.broadcasted_iota(jnp.int32, (128, 128), 0)
    ids_col = lax.broadcasted_iota(jnp.int32, (128, 128), 1)
    ends = jnp.sum(
        jnp.where(ids_col <= ids_row, jnp.broadcast_to(lens[...], (128, 128)), 0).astype(F32),
        axis=1,
        keepdims=True,
    ).astype(jnp.int32)
    place = c * tokens + ids_col
    starts = jnp.max(jnp.where(ends <= place, ends, 0).astype(F32), axis=0, keepdims=True)
    starts = starts.astype(jnp.int32) - c * tokens
    starts = jnp.concatenate([starts] * 2, axis=1)

    for r in range(heads):
        cols, rows = slice(r * d, (r + 1) * d), slice(r * tokens, (r + 1) * tokens)
        q_loads[r].wait()
        q_cols[:, cols] = q_rows[rows, :].T
        g_loads[r].wait()
        g_cols[:, cols] = g_rows[rows, :].T

    for copy in y_copies:
        copy.wait_recv()
    c_copies = [
        send(
            kv.at[OWN], kv.at[role], c_send.at[role], c_recv.at[role], (to, h),
            has_to[role], has_from[role],
        )
        for role, to in ((FAR, c + 4), (CROSS, cross_to), (NEAR, c + 2))
    ]

    chunk = 2 * tokens
    chunks = width // chunk
    key_ids = lax.broadcasted_iota(jnp.int32, (tokens, chunk), 0)
    query_ids = lax.rem(lax.broadcasted_iota(jnp.int32, (tokens, chunk), 1), tokens)
    back_by = [0, 2, 4, 5 - 4 * core, 1 + 2 * core, 3 + 2 * core]
    tops, totals, deltas = {}, {}, {}

    def forward(role):
        k_block = kv[role, :, 0].reshape(tokens, d)
        v_block = kv[role, :, 1].reshape(tokens, d)
        cols = slice(role * tokens, (role + 1) * tokens)
        k_cols[:, cols] = k_block.T
        v_cols[:, cols] = v_block.T
        visible = key_ids - back_by[role] * tokens >= starts
        if role == OWN:
            visible = visible & (key_ids <= query_ids)
        for j in range(chunks):
            qs = slice(j * chunk, (j + 1) * chunk)
            scores = jnp.dot(k_block, q_cols[:, qs], preferred_element_type=F32)
            scores = jnp.where(visible, scores, big_negative)
            top = jnp.max(scores, axis=0, keepdims=True)
            grown = jnp.exp2((scores - top) * (SCALE * LOG2E))
            dp = jnp.dot(v_block, g_cols[:, qs], preferred_element_type=F32)
            tops[role, j] = top
            totals[role, j] = jnp.sum(grown, axis=0, keepdims=True)
            deltas[role, j] = jnp.sum(grown * dp, axis=0, keepdims=True)
            probs[cols, qs] = grown.astype(BF16)
            dprobs[cols, qs] = dp

    forward(OWN)
    c_copies[2].wait_recv()
    c_copies.append(
        send(kv.at[NEAR], kv.at[NEAR_SIB], c_send.at[NEAR_SIB], c_recv.at[NEAR_SIB], (sibling, h))
    )
    c_copies[0].wait_recv()
    c_copies.append(
        send(kv.at[FAR], kv.at[FAR_SIB], c_send.at[FAR_SIB], c_recv.at[FAR_SIB], (sibling, h))
    )
    forward(NEAR)
    forward(FAR)
    c_copies[1].wait_recv()
    forward(CROSS)
    c_copies[3].wait_recv()
    forward(NEAR_SIB)
    c_copies[4].wait_recv()
    forward(FAR_SIB)

    factors, delta = {}, {}
    for j in range(chunks):
        top = functools.reduce(jnp.maximum, [tops[role, j] for role in range(ROLES)])
        lift = [jnp.exp2((tops[role, j] - top) * (SCALE * LOG2E)) for role in range(ROLES)]
        total = sum(lift[role] * totals[role, j] for role in range(ROLES))
        for role in range(ROLES):
            factors[role, j] = lift[role] / total
        delta[j] = sum(factors[role, j] * deltas[role, j] for role in range(ROLES))

    def backward(role):
        rows = slice(role * tokens, (role + 1) * tokens)
        for j in range(chunks):
            qs = slice(j * chunk, (j + 1) * chunk)
            p = probs[rows, qs].astype(F32) * factors[role, j]
            probs[rows, qs] = p.astype(BF16)
            dscores[rows, qs] = (p * (dprobs[rows, qs] - delta[j])).astype(BF16)
        dk_part = jnp.dot(dscores[rows, :], q_rows[...], preferred_element_type=F32) * SCALE
        dv_part = jnp.dot(probs[rows, :], g_rows[...], preferred_element_type=F32)
        return dk_part, dv_part

    def put(where, dk_part, dv_part):
        where[:, 0] = dk_part.astype(BF16).reshape(n_head, piece, d)
        where[:, 1] = dv_part.astype(BF16).reshape(n_head, piece, d)

    def with_back(slot, dk_part, dv_part):
        dk_part = dk_part + back[slot, :, 0].reshape(tokens, d).astype(F32)
        dv_part = dv_part + back[slot, :, 1].reshape(tokens, d).astype(F32)
        return dk_part, dv_part

    b_copies = {}

    def send_back(role, to):
        b_copies[role] = send(
            part.at[role], back.at[role], b_send.at[role], b_recv.at[role], (to, h),
            has_from.get(role), has_to.get(role),
        )

    put(part.at[FAR_SIB], *backward(FAR_SIB))
    send_back(FAR_SIB, sibling)
    put(part.at[NEAR_SIB], *backward(NEAR_SIB))
    send_back(NEAR_SIB, sibling)
    put(part.at[CROSS], *backward(CROSS))
    send_back(CROSS, cross_from)
    far_grads = backward(FAR)
    b_copies[FAR_SIB].wait_recv()
    put(part.at[FAR], *with_back(FAR_SIB, *far_grads))
    send_back(FAR, c - 4)
    near_grads = backward(NEAR)
    b_copies[NEAR_SIB].wait_recv()
    put(part.at[NEAR], *with_back(NEAR_SIB, *near_grads))
    send_back(NEAR, c - 2)
    own_grads = backward(OWN)

    for j in range(chunks):
        qs = slice(j * chunk, (j + 1) * chunk)
        out = jnp.dot(v_cols[...], probs[:, qs], preferred_element_type=F32).astype(BF16)
        grad = jnp.dot(k_cols[...], dscores[:, qs], preferred_element_type=F32) * SCALE
        grad = grad.astype(BF16)
        for i in range(chunk // tokens):
            r = j * (chunk // tokens) + i
            att[:, r * d : (r + 1) * d] = out[:, i * tokens : (i + 1) * tokens].T
            dq[:, r * d : (r + 1) * d] = grad[:, i * tokens : (i + 1) * tokens].T
    for role in (CROSS, NEAR, FAR):
        b_copies[role].wait_recv()
        own_grads = with_back(role, *own_grads)
    put(grad_stage, *own_grads)
    z_copies = []
    for step in range(1, n_head):
        to = lax.rem(h + step, n_head)
        z_copies.append(
            send(grad_stage.at[to], grad_in.at[h], z_send.at[step], z_recv.at[step], (c, to))
        )
    grad_in[h] = grad_stage[h]
    for copy in z_copies:
        copy.wait_recv()
    for r in range(n_head):
        dk_out[:, r * d : (r + 1) * d] = grad_in[r, 0]
        dv_out[:, r * d : (r + 1) * d] = grad_in[r, 1]

    for copy in y_copies + c_copies + list(b_copies.values()) + z_copies:
        copy.wait_send()


def per_device(n_ctx, n_head, queries, keys, values, output_gradient, doc_lengths):
    tokens = queries.shape[0]
    piece = keys.shape[0]
    d = HEAD_SIZE
    heads = queries.shape[1] // d
    width = heads * tokens
    docs = doc_lengths.shape[0]
    hbm_spec = pl.BlockSpec(memory_space=pltpu.HBM)
    vmem_spec = pl.BlockSpec(memory_space=pltpu.VMEM)
    block = (n_head, 2, piece, d)
    dma = pltpu.SemaphoreType.DMA
    return pl.pallas_call(
        functools.partial(kernel, n_ctx, n_head, tokens, heads),
        out_shape=(
            jax.ShapeDtypeStruct(queries.shape, BF16),
            jax.ShapeDtypeStruct(queries.shape, BF16),
            jax.ShapeDtypeStruct(keys.shape, BF16),
            jax.ShapeDtypeStruct(values.shape, BF16),
        ),
        in_specs=[hbm_spec] * 5,
        out_specs=(vmem_spec,) * 4,
        scratch_shapes=[
            pltpu.VMEM(keys.shape, BF16),
            pltpu.VMEM(values.shape, BF16),
            pltpu.VMEM((1, docs), jnp.int32),
            pltpu.VMEM((width, d), BF16),
            pltpu.VMEM((width, d), BF16),
            pltpu.VMEM((d, width), BF16),
            pltpu.VMEM((d, width), BF16),
            pltpu.VMEM(block, BF16),
            pltpu.VMEM((ROLES, *block), BF16),
            pltpu.VMEM((d, ROLES * tokens), BF16),
            pltpu.VMEM((d, ROLES * tokens), BF16),
            pltpu.VMEM((ROLES * tokens, width), BF16),
            pltpu.VMEM((ROLES * tokens, width), F32),
            pltpu.VMEM((ROLES * tokens, width), BF16),
            pltpu.VMEM((ROLES, *block), BF16),
            pltpu.VMEM((ROLES, *block), BF16),
            pltpu.VMEM(block, BF16),
            pltpu.VMEM(block, BF16),
            dma((3 + 2 * heads,)),
            dma((n_head,)),
            dma((n_head,)),
            dma((ROLES,)),
            dma((ROLES,)),
            dma((ROLES,)),
            dma((ROLES,)),
            dma((n_head,)),
            dma((n_head,)),
        ],
        compiler_params=pltpu.CompilerParams(
            collective_id=0, has_side_effects=True, vmem_limit_bytes=40 * 1024 * 1024
        ),
    )(*(
        pltpu.with_memory_space_constraint(x, pltpu.HBM)
        for x in (queries, keys, values, output_gradient, doc_lengths.reshape(1, docs))
    ))


def solution(mesh):
    n_ctx, n_head = mesh.shape["ctx"], mesh.shape["head"]
    return jax.shard_map(
        functools.partial(per_device, n_ctx, n_head),
        mesh=mesh,
        in_specs=(
            P("ctx", "head"),
            P(("ctx", "head"), None),
            P(("ctx", "head"), None),
            P("ctx", "head"),
            P(),
        ),
        out_specs=(
            P("ctx", "head"),
            P("ctx", "head"),
            P(("ctx", "head"), None),
            P(("ctx", "head"), None),
        ),
        check_vma=False,
    )
```

```python
import functools

import jax
import jax.numpy as jnp
from jax import lax
from jax.experimental import pallas as pl
from jax.experimental.pallas import tpu as pltpu
from jax.sharding import PartitionSpec as P

HEAD_SIZE = 128
SCALE = HEAD_SIZE ** (-0.5)
LOG2E = 1.4426950408889634
big_negative = -1e30
MESH = pl.DeviceIdType.MESH
F32 = jnp.float32
BF16 = jnp.bfloat16

OWN = 0
NEAR = 1
FAR = 2
CROSS = 3
NEAR_SIB = 4
FAR_SIB = 5
ROLES = 6


def ring_steps(n):
    return sorted(range(n), key=lambda step: (min(step, n - step), step))


class Message:
    def __init__(self, src, dst, send_sem, recv_sem, to, sends=None, receives=None):
        self.copy = pltpu.make_async_remote_copy(
            src_ref=src,
            dst_ref=dst,
            send_sem=send_sem,
            recv_sem=recv_sem,
            device_id=to,
            device_id_type=MESH,
        )
        self.sends, self.receives = sends, receives

    def start(self):
        run_if(self.sends, self.copy.start)

    def wait_recv(self):
        run_if(self.receives, self.copy.wait_recv)

    def wait_send(self):
        run_if(self.sends, self.copy.wait_send)


def run_if(condition, action):
    if condition is None:
        action()
        return

    @pl.when(condition)
    def _():
        action()


def kernel(
    n_ctx,
    n_head,
    tokens,
    heads,
    q_hbm,
    k_hbm,
    v_hbm,
    g_hbm,
    len_hbm,
    att,
    dq,
    dk_out,
    dv_out,
    k_in,
    v_in,
    lens,
    q_in,
    g_in,
    q_cols,
    g_cols,
    kv_stage,
    kv,
    k_cols,
    v_cols,
    probs,
    dprobs,
    dscores,
    part,
    back,
    grad_stage,
    grad_in,
    in_sem,
    y_send,
    y_recv,
    c_send,
    c_recv,
    b_send,
    b_recv,
    z_send,
    z_recv,
):
    d = HEAD_SIZE
    c = lax.axis_index("ctx")
    h = lax.axis_index("head")
    core = lax.rem(c, 2)
    piece = tokens // n_head
    width = heads * tokens
    steps = ring_steps(n_head)
    near_slots = n_head // 2 + 1
    groups = (pl.ds(0, near_slots * 2 * piece), pl.ds(near_slots * 2 * piece, (n_head - near_slots) * 2 * piece))

    def slot_rows(slot):
        return pl.ds(slot * 2 * piece, 2 * piece)

    sibling = c + 1 - 2 * core
    cross_to = c + 1 + 4 * core
    cross_from = c + 4 * core - 5
    has_from = {NEAR: c >= 2, FAR: c >= 4, CROSS: cross_from >= 0}
    has_to = {NEAR: c + 2 < n_ctx, FAR: c + 4 < n_ctx, CROSS: cross_to < n_ctx}

    loads = [
        pltpu.make_async_copy(source, target, in_sem.at[i])
        for i, (source, target) in enumerate(
            ((k_hbm, k_in), (v_hbm, v_in), (len_hbm, lens), (q_hbm, q_in), (g_hbm, g_in))
        )
    ]
    loads[0].start()
    loads[1].start()

    barrier = pltpu.get_barrier_semaphore()

    def greet(peer):
        pl.semaphore_signal(barrier, inc=1, device_id=peer, device_id_type=MESH)

    for step in range(1, n_head):
        greet((c, lax.rem(h + step, n_head)))
    greet((sibling, h))
    n_peers = n_head
    far_cross = jnp.where(core == 0, cross_from, cross_to)
    for there, peer in (
        (has_from[NEAR], c - 2),
        (has_to[NEAR], c + 2),
        (has_from[FAR], c - 4),
        (has_to[FAR], c + 4),
        ((far_cross >= 0) & (far_cross < n_ctx), far_cross),
    ):

        @pl.when(there)
        def _(peer=peer):
            greet((peer, h))

        n_peers = n_peers + jnp.where(there, 1, 0)

    for load in loads[2:]:
        load.start()
    loads[0].wait()
    loads[1].wait()
    for r in range(n_head):
        cols = slice(r * d, (r + 1) * d)
        kv_stage[r, :piece] = k_in[:, cols]
        kv_stage[r, piece:] = v_in[:, cols]
    kv[OWN, slot_rows(0)] = kv_stage[h]
    pl.semaphore_wait(barrier, n_peers)

    def send(src, dst, send_sem, recv_sem, to, sends=None, receives=None):
        copy = Message(src, dst, send_sem, recv_sem, to, sends, receives)
        copy.start()
        return copy

    y_copies = {}
    for step in reversed(steps[1:]):
        to, slot = lax.rem(h + step, n_head), steps.index(n_head - step)
        y_copies[slot] = send(
            kv_stage.at[to], kv.at[OWN, slot_rows(slot)], y_send.at[slot], y_recv.at[slot], (c, to)
        )

    for role in (NEAR, FAR, CROSS):

        @pl.when(jnp.logical_not(has_from[role]))
        def _(role=role):
            kv[role] = jnp.zeros(kv.shape[1:], BF16)

        @pl.when(jnp.logical_not(has_to[role]))
        def _(role=role):
            back[role] = jnp.zeros(back.shape[1:], BF16)

    loads[2].wait()
    ids_row = lax.broadcasted_iota(jnp.int32, (128, 128), 0)
    ids_col = lax.broadcasted_iota(jnp.int32, (128, 128), 1)
    ends = jnp.sum(
        jnp.where(ids_col <= ids_row, jnp.broadcast_to(lens[...], (128, 128)), 0).astype(F32),
        axis=1,
        keepdims=True,
    ).astype(jnp.int32)
    place = c * tokens + ids_col
    starts = jnp.max(jnp.where(ends <= place, ends, 0).astype(F32), axis=0, keepdims=True)
    starts = starts.astype(jnp.int32) - c * tokens
    starts = jnp.concatenate([starts] * 2, axis=1)

    c_copies = {}

    def send_on(source, role, to, group):
        rows = groups[group]
        c_copies[role, group] = send(
            kv.at[source, rows],
            kv.at[role, rows],
            c_send.at[role, group],
            c_recv.at[role, group],
            (to, h),
            has_to.get(role),
            has_from.get(role),
        )

    for group, slots in enumerate((range(1, near_slots), range(near_slots, n_head))):
        for slot in slots:
            y_copies[slot].wait_recv()
        for role, to in ((FAR, c + 4), (CROSS, cross_to), (NEAR, c + 2)):
            send_on(OWN, role, to, group)

    loads[3].wait()
    loads[4].wait()
    for r in range(heads):
        cols = slice(r * d, (r + 1) * d)
        q_cols[:, cols] = q_in[:, cols].T
        g_cols[:, cols] = g_in[:, cols].T

    chunk = 2 * tokens
    chunks = width // chunk
    key_rows = lax.broadcasted_iota(jnp.int32, (tokens, chunk), 0)
    key_slots = key_rows // piece
    key_steps = jnp.where(key_slots % 2 == 1, (key_slots + 1) // 2, n_head - key_slots // 2)
    key_ids = lax.rem(h + key_steps, n_head) * piece + lax.rem(key_rows, piece)
    query_ids = lax.rem(lax.broadcasted_iota(jnp.int32, (tokens, chunk), 1), tokens)
    back_by = [0, 2, 4, 5 - 4 * core, 1 + 2 * core, 3 + 2 * core]
    tops, totals, deltas = {}, {}, {}

    def apart(both):
        both = both.reshape(n_head, 2, piece, d)
        return both[:, 0].reshape(tokens, d), both[:, 1].reshape(tokens, d)

    def forward(role):
        k_block, v_block = apart(kv[role])
        cols = slice(role * tokens, (role + 1) * tokens)
        k_cols[:, cols] = k_block.T
        v_cols[:, cols] = v_block.T
        visible = key_ids - back_by[role] * tokens >= starts
        if role == OWN:
            visible = visible & (key_ids <= query_ids)
        for j in range(chunks):
            qs = slice(j * chunk, (j + 1) * chunk)
            scores = jnp.dot(k_block, q_cols[:, qs], preferred_element_type=F32)
            scores = jnp.where(visible, scores, big_negative)
            top = jnp.max(scores, axis=0, keepdims=True)
            grown = jnp.exp2((scores - top) * (SCALE * LOG2E))
            dp = jnp.dot(v_block, g_cols[:, qs], preferred_element_type=F32)
            tops[role, j] = top
            totals[role, j] = jnp.sum(grown, axis=0, keepdims=True)
            deltas[role, j] = jnp.sum(grown * dp, axis=0, keepdims=True)
            probs[cols, qs] = grown.astype(BF16)
            dprobs[cols, qs] = dp

    forward(OWN)
    for group in range(2):
        for role, there in ((NEAR, NEAR_SIB), (FAR, FAR_SIB)):
            c_copies[role, group].wait_recv()
            send_on(role, there, sibling, group)
    forward(NEAR)
    forward(FAR)
    for role in (CROSS, NEAR_SIB, FAR_SIB):
        for group in range(2):
            c_copies[role, group].wait_recv()
        forward(role)

    factors, delta = {}, {}
    for j in range(chunks):
        top = functools.reduce(jnp.maximum, [tops[role, j] for role in range(ROLES)])
        lift = [jnp.exp2((tops[role, j] - top) * (SCALE * LOG2E)) for role in range(ROLES)]
        total = sum(lift[role] * totals[role, j] for role in range(ROLES))
        for role in range(ROLES):
            factors[role, j] = lift[role] / total
        delta[j] = sum(factors[role, j] * deltas[role, j] for role in range(ROLES))

    def backward(role):
        rows = slice(role * tokens, (role + 1) * tokens)
        dk_part = dv_part = 0.0
        for j in range(chunks):
            qs = slice(j * chunk, (j + 1) * chunk)
            p = probs[rows, qs].astype(F32) * factors[role, j]
            ds = (p * (dprobs[rows, qs] - delta[j])).astype(BF16)
            p = p.astype(BF16)
            probs[rows, qs] = p
            dscores[rows, qs] = ds
            dk_part += jnp.dot(ds, by_rows(q_in, j), preferred_element_type=F32)
            dv_part += jnp.dot(p, by_rows(g_in, j), preferred_element_type=F32)
        return dk_part * SCALE, dv_part

    def by_rows(ref, j):
        pair = [
            ref[:, r * d : (r + 1) * d]
            for r in range(j * chunk // tokens, (j + 1) * chunk // tokens)
        ]
        return jnp.concatenate(pair, axis=0)

    def together(dk_part, dv_part, dtype):
        pieces = [x.astype(dtype).reshape(n_head, 1, piece, d) for x in (dk_part, dv_part)]
        return jnp.concatenate(pieces, axis=1).reshape(2 * tokens, d)

    def put(where, dk_part, dv_part):
        where[...] = together(dk_part, dv_part, BF16)

    def with_back(role, dk_part, dv_part):
        for group in range(2):
            b_copies[role, group].wait_recv()
        dk_back, dv_back = apart(back[role])
        return dk_part + dk_back.astype(F32), dv_part + dv_back.astype(F32)

    b_copies = {}

    def send_back(role, to):
        for group in (1, 0):
            rows = groups[group]
            b_copies[role, group] = send(
                part.at[role, rows],
                back.at[role, rows],
                b_send.at[role, group],
                b_recv.at[role, group],
                (to, h),
                has_from.get(role),
                has_to.get(role),
            )

    put(part.at[FAR_SIB], *backward(FAR_SIB))
    send_back(FAR_SIB, sibling)
    put(part.at[NEAR_SIB], *backward(NEAR_SIB))
    send_back(NEAR_SIB, sibling)
    put(part.at[CROSS], *backward(CROSS))
    send_back(CROSS, cross_from)
    far_grads = backward(FAR)
    put(part.at[FAR], *with_back(FAR_SIB, *far_grads))
    send_back(FAR, c - 4)
    near_grads = backward(NEAR)
    put(part.at[NEAR], *with_back(NEAR_SIB, *near_grads))
    send_back(NEAR, c - 2)
    own_grads = backward(OWN)

    for j in range(chunks):
        qs = slice(j * chunk, (j + 1) * chunk)
        out = jnp.dot(v_cols[...], probs[:, qs], preferred_element_type=F32).astype(BF16)
        grad = jnp.dot(k_cols[...], dscores[:, qs], preferred_element_type=F32) * SCALE
        grad = grad.astype(BF16)
        for i in range(chunk // tokens):
            r = j * (chunk // tokens) + i
            att[:, r * d : (r + 1) * d] = out[:, i * tokens : (i + 1) * tokens].T
            dq[:, r * d : (r + 1) * d] = grad[:, i * tokens : (i + 1) * tokens].T
    for copy in list(y_copies.values()) + list(c_copies.values()):
        copy.wait_send()
    own_sum = together(*own_grads, F32)
    z_copies = {}
    for group, slots in ((1, range(near_slots, n_head)), (0, range(near_slots))):
        rows = slice(groups[group].start, groups[group].start + groups[group].size)
        for role in (CROSS, FAR, NEAR):
            b_copies[role, group].wait_recv()
        total = own_sum[rows]
        for role in (CROSS, FAR, NEAR):
            total += back[role, rows].astype(F32)
        grad_stage[rows] = total.astype(BF16)
        for slot in reversed(slots):
            if slot:
                to = lax.rem(h + steps[slot], n_head)
                z_copies[slot] = send(
                    grad_stage.at[slot_rows(slot)],
                    grad_in.at[h],
                    z_send.at[slot],
                    z_recv.at[slot],
                    (c, to),
                )
    grad_in[h] = grad_stage[slot_rows(0)]
    for copy in b_copies.values():
        copy.wait_send()
    for copy in z_copies.values():
        copy.wait_recv()
    for r in range(n_head):
        dk_out[:, r * d : (r + 1) * d] = grad_in[r, :piece]
        dv_out[:, r * d : (r + 1) * d] = grad_in[r, piece:]

    for copy in z_copies.values():
        copy.wait_send()


def write_out(*refs):
    for i in range(4):
        refs[4 + i][...] = refs[i][...]


def per_device(n_ctx, n_head, queries, keys, values, output_gradient, doc_lengths):
    tokens = queries.shape[0]
    piece = keys.shape[0]
    d = HEAD_SIZE
    heads = queries.shape[1] // d
    width = heads * tokens
    docs = doc_lengths.shape[0]
    hbm_spec = pl.BlockSpec(memory_space=pltpu.HBM)
    vmem_spec = pl.BlockSpec(memory_space=pltpu.VMEM)
    block = (2 * tokens, d)
    dma = pltpu.SemaphoreType.DMA
    results = pl.pallas_call(
        functools.partial(kernel, n_ctx, n_head, tokens, heads),
        out_shape=(
            jax.ShapeDtypeStruct(queries.shape, BF16),
            jax.ShapeDtypeStruct(queries.shape, BF16),
            jax.ShapeDtypeStruct(keys.shape, BF16),
            jax.ShapeDtypeStruct(values.shape, BF16),
        ),
        in_specs=[hbm_spec] * 5,
        out_specs=(vmem_spec,) * 4,
        scratch_shapes=[
            pltpu.VMEM(keys.shape, BF16),
            pltpu.VMEM(values.shape, BF16),
            pltpu.VMEM((1, docs), jnp.int32),
            pltpu.VMEM((tokens, width), BF16),
            pltpu.VMEM((tokens, width), BF16),
            pltpu.VMEM((d, width), BF16),
            pltpu.VMEM((d, width), BF16),
            pltpu.VMEM((n_head, 2 * piece, d), BF16),
            pltpu.VMEM((ROLES, *block), BF16),
            pltpu.VMEM((d, ROLES * tokens), BF16),
            pltpu.VMEM((d, ROLES * tokens), BF16),
            pltpu.VMEM((ROLES * tokens, width), BF16),
            pltpu.VMEM((ROLES * tokens, width), F32),
            pltpu.VMEM((ROLES * tokens, width), BF16),
            pltpu.VMEM((ROLES, *block), BF16),
            pltpu.VMEM((ROLES, *block), BF16),
            pltpu.VMEM(block, BF16),
            pltpu.VMEM((n_head, 2 * piece, d), BF16),
            dma((5,)),
            dma((n_head,)),
            dma((n_head,)),
            dma((ROLES, 2)),
            dma((ROLES, 2)),
            dma((ROLES, 2)),
            dma((ROLES, 2)),
            dma((n_head,)),
            dma((n_head,)),
        ],
        compiler_params=pltpu.CompilerParams(
            collective_id=0, has_side_effects=True, vmem_limit_bytes=40 * 1024 * 1024
        ),
    )(*(
        pltpu.with_memory_space_constraint(x, pltpu.HBM)
        for x in (queries, keys, values, output_gradient, doc_lengths.reshape(1, docs))
    ))
    return pl.pallas_call(
        write_out,
        out_shape=tuple(jax.ShapeDtypeStruct(x.shape, x.dtype) for x in results),
        in_specs=[vmem_spec] * 4,
        out_specs=(vmem_spec,) * 4,
        scratch_shapes=[dma((4,))],
        compiler_params=pltpu.CompilerParams(vmem_limit_bytes=8 * 1024 * 1024),
    )(*results)


def solution(mesh):
    n_ctx, n_head = mesh.shape["ctx"], mesh.shape["head"]
    return jax.shard_map(
        functools.partial(per_device, n_ctx, n_head),
        mesh=mesh,
        in_specs=(
            P("ctx", "head"),
            P(("ctx", "head"), None),
            P(("ctx", "head"), None),
            P("ctx", "head"),
            P(),
        ),
        out_specs=(
            P("ctx", "head"),
            P("ctx", "head"),
            P(("ctx", "head"), None),
            P(("ctx", "head"), None),
        ),
        check_vma=False,
    )
```

```python
import functools

import jax
import jax.numpy as jnp
from jax import lax
from jax.experimental import pallas as pl
from jax.experimental.pallas import tpu as pltpu
from jax.sharding import PartitionSpec as P

HEAD_SIZE = 128
SCALE = HEAD_SIZE ** (-0.5)
LOG2E = 1.4426950408889634
big_negative = -1e30
MESH = pl.DeviceIdType.MESH
F32 = jnp.float32
BF16 = jnp.bfloat16

OWN = 0
NEAR = 1
FAR = 2
CROSS = 3
NEAR_SIB = 4
FAR_SIB = 5
ROLES = 6


def ring_steps(n):
    return sorted(range(n), key=lambda step: (min(step, n - step), step))


class Message:
    def __init__(self, src, dst, send_sem, recv_sem, to, sends=None, receives=None):
        self.copy = pltpu.make_async_remote_copy(
            src_ref=src,
            dst_ref=dst,
            send_sem=send_sem,
            recv_sem=recv_sem,
            device_id=to,
            device_id_type=MESH,
        )
        self.sends, self.receives = sends, receives

    def start(self):
        run_if(self.sends, self.copy.start)

    def wait_recv(self):
        run_if(self.receives, self.copy.wait_recv)

    def wait_send(self):
        run_if(self.sends, self.copy.wait_send)


def run_if(condition, action):
    if condition is None:
        action()
        return

    @pl.when(condition)
    def _():
        action()


def kernel(
    n_ctx,
    n_head,
    tokens,
    heads,
    q_hbm,
    k_hbm,
    v_hbm,
    g_hbm,
    len_hbm,
    att,
    dq,
    dk_out,
    dv_out,
    k_in,
    v_in,
    lens,
    q_in,
    g_in,
    q_cols,
    g_cols,
    kv_stage,
    kv,
    k_cols,
    v_cols,
    probs,
    dprobs,
    dscores,
    part,
    back,
    grad_stage,
    grad_in,
    in_sem,
    y_send,
    y_recv,
    c_send,
    c_recv,
    b_send,
    b_recv,
    z_send,
    z_recv,
    ready,
):
    d = HEAD_SIZE
    c = lax.axis_index("ctx")
    h = lax.axis_index("head")
    core = lax.rem(c, 2)
    piece = tokens // n_head
    width = heads * tokens
    steps = ring_steps(n_head)
    near_slots = n_head // 2 + 1
    groups = (pl.ds(0, near_slots * 2 * piece), pl.ds(near_slots * 2 * piece, (n_head - near_slots) * 2 * piece))

    def slot_rows(slot):
        return pl.ds(slot * 2 * piece, 2 * piece)

    sibling = c + 1 - 2 * core
    cross_to = c + 1 + 4 * core
    cross_from = c + 4 * core - 5
    has_from = {NEAR: c >= 2, FAR: c >= 4, CROSS: cross_from >= 0}
    has_to = {NEAR: c + 2 < n_ctx, FAR: c + 4 < n_ctx, CROSS: cross_to < n_ctx}

    loads = [
        pltpu.make_async_copy(source, target, in_sem.at[i])
        for i, (source, target) in enumerate(
            ((k_hbm, k_in), (v_hbm, v_in), (len_hbm, lens), (q_hbm, q_in), (g_hbm, g_in))
        )
    ]
    barrier = pltpu.get_barrier_semaphore()

    def greet(peer):
        pl.semaphore_signal(barrier, inc=1, device_id=peer, device_id_type=MESH)

    for step in reversed(steps[1:]):
        greet((c, lax.rem(h + step, n_head)))
    later = ((has_to[FAR], c + 4), (has_to[CROSS] & (core == 1), cross_to), (has_to[NEAR], c + 2))
    earlier = (
        (has_from[FAR], c - 4),
        (has_from[CROSS] & (core == 0), cross_from),
        (has_from[NEAR], c - 2),
    )
    for there, peer in later:
        run_if(there, functools.partial(greet, (peer, h)))
    greet((sibling, h))
    n_later = sum(jnp.where(there, 1, 0) for there, _ in later)
    n_earlier = sum(jnp.where(there, 1, 0) for there, _ in earlier)

    loads[0].start()
    loads[1].start()
    for load in loads[2:]:
        load.start()
    loads[0].wait()
    loads[1].wait()
    for r in range(n_head):
        cols = slice(r * d, (r + 1) * d)
        kv_stage[r, :piece] = k_in[:, cols]
        kv_stage[r, piece:] = v_in[:, cols]
    kv[OWN, slot_rows(0)] = kv_stage[h]
    pl.semaphore_wait(barrier, n_head + n_earlier)

    def send(src, dst, send_sem, recv_sem, to, sends=None, receives=None):
        copy = Message(src, dst, send_sem, recv_sem, to, sends, receives)
        copy.start()
        return copy

    y_copies = {}
    for step in reversed(steps[1:]):
        to, slot = lax.rem(h + step, n_head), steps.index(n_head - step)
        y_copies[slot] = send(
            kv_stage.at[to], kv.at[OWN, slot_rows(slot)], y_send.at[slot], y_recv.at[slot], (c, to)
        )

    def tell(peer):
        pl.semaphore_signal(ready, inc=1, device_id=(peer, h), device_id_type=MESH)

    for there, peer in earlier:
        run_if(there, functools.partial(tell, peer))

    for role in (NEAR, FAR, CROSS):

        @pl.when(jnp.logical_not(has_from[role]))
        def _(role=role):
            kv[role] = jnp.zeros(kv.shape[1:], BF16)

        @pl.when(jnp.logical_not(has_to[role]))
        def _(role=role):
            back[role] = jnp.zeros(back.shape[1:], BF16)

    loads[2].wait()
    ids_row = lax.broadcasted_iota(jnp.int32, (128, 128), 0)
    ids_col = lax.broadcasted_iota(jnp.int32, (128, 128), 1)
    ends = jnp.sum(
        jnp.where(ids_col <= ids_row, jnp.broadcast_to(lens[...], (128, 128)), 0).astype(F32),
        axis=1,
        keepdims=True,
    ).astype(jnp.int32)
    place = c * tokens + ids_col
    starts = jnp.max(jnp.where(ends <= place, ends, 0).astype(F32), axis=0, keepdims=True)
    starts = starts.astype(jnp.int32) - c * tokens
    starts = jnp.concatenate([starts] * 2, axis=1)

    c_copies = {}

    def send_on(source, role, to, group):
        rows = groups[group]
        c_copies[role, group] = send(
            kv.at[source, rows],
            kv.at[role, rows],
            c_send.at[role, group],
            c_recv.at[role, group],
            (to, h),
            has_to.get(role),
            has_from.get(role),
        )

    for group, slots in enumerate((range(1, near_slots), range(near_slots, n_head))):
        for slot in slots:
            y_copies[slot].wait_recv()
        if group == 0:
            run_if(n_later > 0, lambda: pl.semaphore_wait(ready, n_later))
        for role, to in ((FAR, c + 4), (CROSS, cross_to), (NEAR, c + 2)):
            send_on(OWN, role, to, group)

    loads[3].wait()
    loads[4].wait()
    for r in range(heads):
        cols = slice(r * d, (r + 1) * d)
        q_cols[:, cols] = q_in[:, cols].T
        g_cols[:, cols] = g_in[:, cols].T

    chunk = 2 * tokens
    chunks = width // chunk
    key_rows = lax.broadcasted_iota(jnp.int32, (tokens, chunk), 0)
    key_slots = key_rows // piece
    key_steps = jnp.where(key_slots % 2 == 1, (key_slots + 1) // 2, n_head - key_slots // 2)
    key_ids = lax.rem(h + key_steps, n_head) * piece + lax.rem(key_rows, piece)
    query_ids = lax.rem(lax.broadcasted_iota(jnp.int32, (tokens, chunk), 1), tokens)
    back_by = [0, 2, 4, 5 - 4 * core, 1 + 2 * core, 3 + 2 * core]
    tops, totals, deltas = {}, {}, {}

    def apart(both):
        both = both.reshape(n_head, 2, piece, d)
        return both[:, 0].reshape(tokens, d), both[:, 1].reshape(tokens, d)

    def forward(*roles):
        first, count = min(roles), len(roles)
        blocks = [apart(kv[role]) for role in range(first, first + count)]
        k_block = jnp.concatenate([block[0] for block in blocks], axis=0)
        v_block = jnp.concatenate([block[1] for block in blocks], axis=0)
        rows = slice(first * tokens, (first + count) * tokens)
        k_cols[:, rows] = k_block.T
        v_cols[:, rows] = v_block.T
        for j in range(chunks):
            qs = slice(j * chunk, (j + 1) * chunk)
            all_scores = jnp.dot(k_block, q_cols[:, qs], preferred_element_type=F32)
            all_dp = jnp.dot(v_block, g_cols[:, qs], preferred_element_type=F32)
            for i in range(count):
                role = first + i
                part_rows = slice(i * tokens, (i + 1) * tokens)
                visible = key_ids - back_by[role] * tokens >= starts
                if role == OWN:
                    visible = visible & (key_ids <= query_ids)
                scores = jnp.where(visible, all_scores[part_rows], big_negative)
                top = jnp.max(scores, axis=0, keepdims=True)
                grown = jnp.exp2((scores - top) * (SCALE * LOG2E))
                dp = all_dp[part_rows]
                tops[role, j] = top
                totals[role, j] = jnp.sum(grown, axis=0, keepdims=True)
                deltas[role, j] = jnp.sum(grown * dp, axis=0, keepdims=True)
                cols = slice(role * tokens, (role + 1) * tokens)
                probs[cols, qs] = grown.astype(BF16)
                dprobs[cols, qs] = dp

    forward(OWN)
    for role, there in ((NEAR, NEAR_SIB), (FAR, FAR_SIB)):
        for group in range(2):
            c_copies[role, group].wait_recv()
            send_on(role, there, sibling, group)
        if role == NEAR:
            forward(NEAR)
    for group in range(2):
        c_copies[CROSS, group].wait_recv()
    forward(FAR, CROSS)
    for role in (NEAR_SIB, FAR_SIB):
        for group in range(2):
            c_copies[role, group].wait_recv()
    forward(NEAR_SIB, FAR_SIB)

    factors, delta = {}, {}
    for j in range(chunks):
        top = functools.reduce(jnp.maximum, [tops[role, j] for role in range(ROLES)])
        lift = [jnp.exp2((tops[role, j] - top) * (SCALE * LOG2E)) for role in range(ROLES)]
        total = sum(lift[role] * totals[role, j] for role in range(ROLES))
        for role in range(ROLES):
            factors[role, j] = lift[role] / total
        delta[j] = sum(factors[role, j] * deltas[role, j] for role in range(ROLES))

    def backward(*roles):
        first, count = min(roles), len(roles)
        dk_part = dv_part = 0.0
        for j in range(chunks):
            qs = slice(j * chunk, (j + 1) * chunk)
            ps, dss = [], []
            for role in range(first, first + count):
                rows = slice(role * tokens, (role + 1) * tokens)
                p = probs[rows, qs].astype(F32) * factors[role, j]
                ds = (p * (dprobs[rows, qs] - delta[j])).astype(BF16)
                p = p.astype(BF16)
                probs[rows, qs] = p
                dscores[rows, qs] = ds
                ps.append(p)
                dss.append(ds)
            dk_part += jnp.dot(
                jnp.concatenate(dss, axis=0), by_rows(q_in, j), preferred_element_type=F32
            )
            dv_part += jnp.dot(
                jnp.concatenate(ps, axis=0), by_rows(g_in, j), preferred_element_type=F32
            )
        cut = [slice(i * tokens, (i + 1) * tokens) for i in range(count)]
        return {first + i: (dk_part[cut[i]] * SCALE, dv_part[cut[i]]) for i in range(count)}

    def by_rows(ref, j):
        pair = [
            ref[:, r * d : (r + 1) * d]
            for r in range(j * chunk // tokens, (j + 1) * chunk // tokens)
        ]
        return jnp.concatenate(pair, axis=0)

    def together(dk_part, dv_part, dtype):
        pieces = [x.astype(dtype).reshape(n_head, 1, piece, d) for x in (dk_part, dv_part)]
        return jnp.concatenate(pieces, axis=1).reshape(2 * tokens, d)

    def put(where, dk_part, dv_part):
        where[...] = together(dk_part, dv_part, BF16)

    def with_back(role, dk_part, dv_part):
        for group in range(2):
            b_copies[role, group].wait_recv()
        dk_back, dv_back = apart(back[role])
        return dk_part + dk_back.astype(F32), dv_part + dv_back.astype(F32)

    b_copies = {}

    def send_back(role, to):
        for group in (1, 0):
            rows = groups[group]
            b_copies[role, group] = send(
                part.at[role, rows],
                back.at[role, rows],
                b_send.at[role, group],
                b_recv.at[role, group],
                (to, h),
                has_from.get(role),
                has_to.get(role),
            )

    grads = backward(NEAR_SIB, FAR_SIB)
    for role in (FAR_SIB, NEAR_SIB):
        put(part.at[role], *grads[role])
        send_back(role, sibling)
    grads = backward(FAR, CROSS)
    put(part.at[CROSS], *grads[CROSS])
    send_back(CROSS, cross_from)
    put(part.at[FAR], *with_back(FAR_SIB, *grads[FAR]))
    send_back(FAR, c - 4)
    grads = backward(OWN, NEAR)
    put(part.at[NEAR], *with_back(NEAR_SIB, *grads[NEAR]))
    send_back(NEAR, c - 2)
    own_grads = grads[OWN]

    for j in range(chunks):
        qs = slice(j * chunk, (j + 1) * chunk)
        out = jnp.dot(v_cols[...], probs[:, qs], preferred_element_type=F32).astype(BF16)
        grad = jnp.dot(k_cols[...], dscores[:, qs], preferred_element_type=F32) * SCALE
        grad = grad.astype(BF16)
        for i in range(chunk // tokens):
            r = j * (chunk // tokens) + i
            att[:, r * d : (r + 1) * d] = out[:, i * tokens : (i + 1) * tokens].T
            dq[:, r * d : (r + 1) * d] = grad[:, i * tokens : (i + 1) * tokens].T
    for copy in list(y_copies.values()) + list(c_copies.values()):
        copy.wait_send()
    own_sum = together(*own_grads, F32)
    z_copies = {}
    for group, slots in ((1, range(near_slots, n_head)), (0, range(near_slots))):
        rows = slice(groups[group].start, groups[group].start + groups[group].size)
        for role in (CROSS, FAR, NEAR):
            b_copies[role, group].wait_recv()
        total = own_sum[rows]
        for role in (CROSS, FAR, NEAR):
            total += back[role, rows].astype(F32)
        grad_stage[rows] = total.astype(BF16)
        for slot in reversed(slots):
            if slot:
                to = lax.rem(h + steps[slot], n_head)
                z_copies[slot] = send(
                    grad_stage.at[slot_rows(slot)],
                    grad_in.at[h],
                    z_send.at[slot],
                    z_recv.at[slot],
                    (c, to),
                )
    grad_in[h] = grad_stage[slot_rows(0)]
    for copy in b_copies.values():
        copy.wait_send()
    for copy in z_copies.values():
        copy.wait_recv()
    for r in range(n_head):
        dk_out[:, r * d : (r + 1) * d] = grad_in[r, :piece]
        dv_out[:, r * d : (r + 1) * d] = grad_in[r, piece:]

    for copy in z_copies.values():
        copy.wait_send()


def write_out(*refs):
    for i in range(4):
        refs[4 + i][...] = refs[i][...]


def per_device(n_ctx, n_head, queries, keys, values, output_gradient, doc_lengths):
    tokens = queries.shape[0]
    piece = keys.shape[0]
    d = HEAD_SIZE
    heads = queries.shape[1] // d
    width = heads * tokens
    docs = doc_lengths.shape[0]
    hbm_spec = pl.BlockSpec(memory_space=pltpu.HBM)
    vmem_spec = pl.BlockSpec(memory_space=pltpu.VMEM)
    block = (2 * tokens, d)
    dma = pltpu.SemaphoreType.DMA
    results = pl.pallas_call(
        functools.partial(kernel, n_ctx, n_head, tokens, heads),
        out_shape=(
            jax.ShapeDtypeStruct(queries.shape, BF16),
            jax.ShapeDtypeStruct(queries.shape, BF16),
            jax.ShapeDtypeStruct(keys.shape, BF16),
            jax.ShapeDtypeStruct(values.shape, BF16),
        ),
        in_specs=[hbm_spec] * 5,
        out_specs=(vmem_spec,) * 4,
        scratch_shapes=[
            pltpu.VMEM(keys.shape, BF16),
            pltpu.VMEM(values.shape, BF16),
            pltpu.VMEM((1, docs), jnp.int32),
            pltpu.VMEM((tokens, width), BF16),
            pltpu.VMEM((tokens, width), BF16),
            pltpu.VMEM((d, width), BF16),
            pltpu.VMEM((d, width), BF16),
            pltpu.VMEM((n_head, 2 * piece, d), BF16),
            pltpu.VMEM((ROLES, *block), BF16),
            pltpu.VMEM((d, ROLES * tokens), BF16),
            pltpu.VMEM((d, ROLES * tokens), BF16),
            pltpu.VMEM((ROLES * tokens, width), BF16),
            pltpu.VMEM((ROLES * tokens, width), F32),
            pltpu.VMEM((ROLES * tokens, width), BF16),
            pltpu.VMEM((ROLES, *block), BF16),
            pltpu.VMEM((ROLES, *block), BF16),
            pltpu.VMEM(block, BF16),
            pltpu.VMEM((n_head, 2 * piece, d), BF16),
            dma((5,)),
            dma((n_head,)),
            dma((n_head,)),
            dma((ROLES, 2)),
            dma((ROLES, 2)),
            dma((ROLES, 2)),
            dma((ROLES, 2)),
            dma((n_head,)),
            dma((n_head,)),
            pltpu.SemaphoreType.REGULAR,
        ],
        compiler_params=pltpu.CompilerParams(
            collective_id=0, has_side_effects=True, vmem_limit_bytes=40 * 1024 * 1024
        ),
    )(*(
        pltpu.with_memory_space_constraint(x, pltpu.HBM)
        for x in (queries, keys, values, output_gradient, doc_lengths.reshape(1, docs))
    ))
    return pl.pallas_call(
        write_out,
        out_shape=tuple(jax.ShapeDtypeStruct(x.shape, x.dtype) for x in results),
        in_specs=[vmem_spec] * 4,
        out_specs=(vmem_spec,) * 4,
        scratch_shapes=[dma((4,))],
        compiler_params=pltpu.CompilerParams(vmem_limit_bytes=8 * 1024 * 1024),
    )(*results)


def solution(mesh):
    n_ctx, n_head = mesh.shape["ctx"], mesh.shape["head"]
    return jax.shard_map(
        functools.partial(per_device, n_ctx, n_head),
        mesh=mesh,
        in_specs=(
            P("ctx", "head"),
            P(("ctx", "head"), None),
            P(("ctx", "head"), None),
            P("ctx", "head"),
            P(),
        ),
        out_specs=(
            P("ctx", "head"),
            P("ctx", "head"),
            P(("ctx", "head"), None),
            P(("ctx", "head"), None),
        ),
        check_vma=False,
    )
```

```python
import functools

import jax
import jax.numpy as jnp
from jax import lax
from jax.experimental import pallas as pl
from jax.experimental.pallas import tpu as pltpu
from jax.sharding import PartitionSpec as P

HEAD_SIZE = 128
SCALE = HEAD_SIZE ** (-0.5)
LOG2E = 1.4426950408889634
big_negative = -1e30
MESH = pl.DeviceIdType.MESH
F32 = jnp.float32
BF16 = jnp.bfloat16

OWN = 0
NEAR = 1
FAR = 2
CROSS = 3
NEAR_SIB = 4
FAR_SIB = 5
ROLES = 6


def ring_steps(n):
    return sorted(range(n), key=lambda step: (min(step, n - step), step))


class Message:
    def __init__(self, src, dst, send_sem, recv_sem, to, sends=None, receives=None):
        self.copy = pltpu.make_async_remote_copy(
            src_ref=src,
            dst_ref=dst,
            send_sem=send_sem,
            recv_sem=recv_sem,
            device_id=to,
            device_id_type=MESH,
        )
        self.sends, self.receives = sends, receives

    def start(self):
        run_if(self.sends, self.copy.start)

    def wait_recv(self):
        run_if(self.receives, self.copy.wait_recv)

    def wait_send(self):
        run_if(self.sends, self.copy.wait_send)


def run_if(condition, action):
    if condition is None:
        action()
        return

    @pl.when(condition)
    def _():
        action()


def kernel(
    n_ctx,
    n_head,
    tokens,
    heads,
    q_hbm,
    k_hbm,
    v_hbm,
    g_hbm,
    len_hbm,
    att,
    dq,
    dk_out,
    dv_out,
    k_in,
    v_in,
    lens,
    q_in,
    g_in,
    q_cols,
    g_cols,
    kv_stage,
    kv,
    k_cols,
    v_cols,
    probs,
    dprobs,
    dscores,
    part,
    back,
    grad_stage,
    grad_in,
    far_in,
    in_sem,
    y_send,
    y_recv,
    c_send,
    c_recv,
    b_send,
    b_recv,
    z_send,
    z_recv,
    f_send,
    f_recv,
    ready,
):
    d = HEAD_SIZE
    c = lax.axis_index("ctx")
    h = lax.axis_index("head")
    core = lax.rem(c, 2)
    piece = tokens // n_head
    width = heads * tokens
    steps = ring_steps(n_head)
    near_slots = n_head // 2 + 1
    back_slots = n_head - 5
    groups = (pl.ds(0, near_slots * 2 * piece), pl.ds(near_slots * 2 * piece, (n_head - near_slots) * 2 * piece))

    def slot_rows(slot):
        return pl.ds(slot * 2 * piece, 2 * piece)

    sibling = c + 1 - 2 * core
    cross_to = c + 1 + 4 * core
    cross_from = c + 4 * core - 5
    has_from = {NEAR: c >= 2, FAR: c >= 4, CROSS: cross_from >= 0}
    has_to = {NEAR: c + 2 < n_ctx, FAR: c + 4 < n_ctx, CROSS: cross_to < n_ctx}

    loads = [
        pltpu.make_async_copy(source, target, in_sem.at[i])
        for i, (source, target) in enumerate(
            ((k_hbm, k_in), (v_hbm, v_in), (len_hbm, lens), (q_hbm, q_in), (g_hbm, g_in))
        )
    ]
    barrier = pltpu.get_barrier_semaphore()

    def greet(peer):
        pl.semaphore_signal(barrier, inc=1, device_id=peer, device_id_type=MESH)

    for step in reversed(steps[1:]):
        greet((c, lax.rem(h + step, n_head)))
    later = ((has_to[FAR], c + 4), (has_to[CROSS] & (core == 1), cross_to), (has_to[NEAR], c + 2))
    earlier = (
        (has_from[FAR], c - 4),
        (has_from[CROSS] & (core == 0), cross_from),
        (has_from[NEAR], c - 2),
    )
    for there, peer in later:
        run_if(there, functools.partial(greet, (peer, h)))
    greet((sibling, h))
    n_later = sum(jnp.where(there, 1, 0) for there, _ in later)
    n_earlier = sum(jnp.where(there, 1, 0) for there, _ in earlier)

    loads[0].start()
    loads[1].start()
    for load in loads[2:]:
        load.start()
    loads[0].wait()
    loads[1].wait()
    for r in range(n_head):
        cols = slice(r * d, (r + 1) * d)
        kv_stage[r, :piece] = k_in[:, cols]
        kv_stage[r, piece:] = v_in[:, cols]
    kv[OWN, slot_rows(0)] = kv_stage[h]
    pl.semaphore_wait(barrier, n_head + n_earlier)

    def send(src, dst, send_sem, recv_sem, to, sends=None, receives=None):
        copy = Message(src, dst, send_sem, recv_sem, to, sends, receives)
        copy.start()
        return copy

    y_copies = {}
    for step in reversed(steps[1:]):
        to, slot = lax.rem(h + step, n_head), steps.index(n_head - step)
        y_copies[slot] = send(
            kv_stage.at[to], kv.at[OWN, slot_rows(slot)], y_send.at[slot], y_recv.at[slot], (c, to)
        )

    def tell(peer):
        pl.semaphore_signal(ready, inc=1, device_id=(peer, h), device_id_type=MESH)

    for there, peer in earlier:
        run_if(there, functools.partial(tell, peer))

    for role in (NEAR, FAR, CROSS):

        @pl.when(jnp.logical_not(has_from[role]))
        def _(role=role):
            kv[role] = jnp.zeros(kv.shape[1:], BF16)

        @pl.when(jnp.logical_not(has_to[role]))
        def _(role=role):
            back[role] = jnp.zeros(back.shape[1:], BF16)
            far_in[role] = jnp.zeros(far_in.shape[1:], BF16)

    loads[2].wait()
    ids_row = lax.broadcasted_iota(jnp.int32, (128, 128), 0)
    ids_col = lax.broadcasted_iota(jnp.int32, (128, 128), 1)
    ends = jnp.sum(
        jnp.where(ids_col <= ids_row, jnp.broadcast_to(lens[...], (128, 128)), 0).astype(F32),
        axis=1,
        keepdims=True,
    ).astype(jnp.int32)
    place = c * tokens + ids_col
    starts = jnp.max(jnp.where(ends <= place, ends, 0).astype(F32), axis=0, keepdims=True)
    starts = starts.astype(jnp.int32) - c * tokens
    starts = jnp.concatenate([starts] * 2, axis=1)

    c_copies = {}

    def send_on(source, role, to, group):
        rows = groups[group]
        c_copies[role, group] = send(
            kv.at[source, rows],
            kv.at[role, rows],
            c_send.at[role, group],
            c_recv.at[role, group],
            (to, h),
            has_to.get(role),
            has_from.get(role),
        )

    for group, slots in enumerate((range(1, near_slots), range(near_slots, n_head))):
        for slot in slots:
            y_copies[slot].wait_recv()
        if group == 0:
            run_if(n_later > 0, lambda: pl.semaphore_wait(ready, n_later))
        for role, to in ((FAR, c + 4), (CROSS, cross_to), (NEAR, c + 2)):
            send_on(OWN, role, to, group)

    loads[3].wait()
    loads[4].wait()
    for r in range(heads):
        cols = slice(r * d, (r + 1) * d)
        q_cols[:, cols] = q_in[:, cols].T
        g_cols[:, cols] = g_in[:, cols].T

    chunk = 2 * tokens
    chunks = width // chunk
    key_rows = lax.broadcasted_iota(jnp.int32, (tokens, chunk), 0)
    key_slots = key_rows // piece
    key_steps = jnp.where(key_slots % 2 == 1, (key_slots + 1) // 2, n_head - key_slots // 2)
    key_ids = lax.rem(h + key_steps, n_head) * piece + lax.rem(key_rows, piece)
    query_ids = lax.rem(lax.broadcasted_iota(jnp.int32, (tokens, chunk), 1), tokens)
    back_by = [0, 2, 4, 5 - 4 * core, 1 + 2 * core, 3 + 2 * core]
    tops, totals, deltas = {}, {}, {}

    def apart(both):
        both = both.reshape(n_head, 2, piece, d)
        return both[:, 0].reshape(tokens, d), both[:, 1].reshape(tokens, d)

    def forward(*roles):
        first, count = min(roles), len(roles)
        blocks = [apart(kv[role]) for role in range(first, first + count)]
        k_block = jnp.concatenate([block[0] for block in blocks], axis=0)
        v_block = jnp.concatenate([block[1] for block in blocks], axis=0)
        rows = slice(first * tokens, (first + count) * tokens)
        k_cols[:, rows] = k_block.T
        v_cols[:, rows] = v_block.T
        for j in range(chunks):
            qs = slice(j * chunk, (j + 1) * chunk)
            all_scores = jnp.dot(k_block, q_cols[:, qs], preferred_element_type=F32)
            all_dp = jnp.dot(v_block, g_cols[:, qs], preferred_element_type=F32)
            for i in range(count):
                role = first + i
                part_rows = slice(i * tokens, (i + 1) * tokens)
                visible = key_ids - back_by[role] * tokens >= starts
                if role == OWN:
                    visible = visible & (key_ids <= query_ids)
                scores = jnp.where(visible, all_scores[part_rows], big_negative)
                top = jnp.max(scores, axis=0, keepdims=True)
                grown = jnp.exp2((scores - top) * (SCALE * LOG2E))
                dp = all_dp[part_rows]
                tops[role, j] = top
                totals[role, j] = jnp.sum(grown, axis=0, keepdims=True)
                deltas[role, j] = jnp.sum(grown * dp, axis=0, keepdims=True)
                cols = slice(role * tokens, (role + 1) * tokens)
                probs[cols, qs] = grown.astype(BF16)
                dprobs[cols, qs] = dp

    forward(OWN)
    for role, there in ((NEAR, NEAR_SIB), (FAR, FAR_SIB)):
        for group in range(2):
            c_copies[role, group].wait_recv()
            send_on(role, there, sibling, group)
        if role == NEAR:
            forward(NEAR)
    for group in range(2):
        c_copies[CROSS, group].wait_recv()
    forward(FAR, CROSS)
    for role in (NEAR_SIB, FAR_SIB):
        for group in range(2):
            c_copies[role, group].wait_recv()
    forward(NEAR_SIB, FAR_SIB)

    factors, delta = {}, {}
    for j in range(chunks):
        top = functools.reduce(jnp.maximum, [tops[role, j] for role in range(ROLES)])
        lift = [jnp.exp2((tops[role, j] - top) * (SCALE * LOG2E)) for role in range(ROLES)]
        total = sum(lift[role] * totals[role, j] for role in range(ROLES))
        for role in range(ROLES):
            factors[role, j] = lift[role] / total
        delta[j] = sum(factors[role, j] * deltas[role, j] for role in range(ROLES))

    def backward(*roles):
        first, count = min(roles), len(roles)
        dk_part = dv_part = 0.0
        for j in range(chunks):
            qs = slice(j * chunk, (j + 1) * chunk)
            ps, dss = [], []
            for role in range(first, first + count):
                rows = slice(role * tokens, (role + 1) * tokens)
                p = probs[rows, qs].astype(F32) * factors[role, j]
                ds = (p * (dprobs[rows, qs] - delta[j])).astype(BF16)
                p = p.astype(BF16)
                probs[rows, qs] = p
                dscores[rows, qs] = ds
                ps.append(p)
                dss.append(ds)
            dk_part += jnp.dot(
                jnp.concatenate(dss, axis=0), by_rows(q_in, j), preferred_element_type=F32
            )
            dv_part += jnp.dot(
                jnp.concatenate(ps, axis=0), by_rows(g_in, j), preferred_element_type=F32
            )
        cut = [slice(i * tokens, (i + 1) * tokens) for i in range(count)]
        return {first + i: (dk_part[cut[i]] * SCALE, dv_part[cut[i]]) for i in range(count)}

    def by_rows(ref, j):
        pair = [
            ref[:, r * d : (r + 1) * d]
            for r in range(j * chunk // tokens, (j + 1) * chunk // tokens)
        ]
        return jnp.concatenate(pair, axis=0)

    def together(dk_part, dv_part, dtype):
        pieces = [x.astype(dtype).reshape(n_head, 1, piece, d) for x in (dk_part, dv_part)]
        return jnp.concatenate(pieces, axis=1).reshape(2 * tokens, d)

    def put(where, dk_part, dv_part):
        where[...] = together(dk_part, dv_part, BF16)

    def with_back(role, dk_part, dv_part):
        b_copies[role].wait_recv()
        dk_back, dv_back = apart(back[role])
        return dk_part + dk_back.astype(F32), dv_part + dv_back.astype(F32)

    b_copies, f_copies = {}, {}

    def send_back(role, to, rows):
        b_copies[role] = send(
            part.at[role, rows],
            back.at[role, rows],
            b_send.at[role],
            b_recv.at[role],
            (to, h),
            has_from.get(role),
            has_to.get(role),
        )

    def send_far(role, to):
        for slot in reversed(range(back_slots, n_head)):
            f_copies[role, slot] = send(
                part.at[role, slot_rows(slot)],
                far_in.at[role, slot],
                f_send.at[role, slot],
                f_recv.at[role, slot],
                (to, lax.rem(h + steps[slot], n_head)),
                has_from.get(role),
                has_to.get(role),
            )

    whole = pl.ds(0, 2 * tokens)
    grads = backward(NEAR_SIB, FAR_SIB)
    for role in (FAR_SIB, NEAR_SIB):
        put(part.at[role], *grads[role])
        send_back(role, sibling, whole)
    grads = backward(FAR, CROSS)
    put(part.at[CROSS], *grads[CROSS])
    send_far(CROSS, cross_from)
    send_back(CROSS, cross_from, pl.ds(0, back_slots * 2 * piece))
    put(part.at[FAR], *with_back(FAR_SIB, *grads[FAR]))
    send_far(FAR, c - 4)
    send_back(FAR, c - 4, pl.ds(0, back_slots * 2 * piece))
    grads = backward(OWN, NEAR)
    put(part.at[NEAR], *with_back(NEAR_SIB, *grads[NEAR]))
    send_far(NEAR, c - 2)
    send_back(NEAR, c - 2, pl.ds(0, back_slots * 2 * piece))
    put(part.at[OWN], *grads[OWN])
    send_far(OWN, c)
    own_grads = grads[OWN]

    for j in range(chunks):
        qs = slice(j * chunk, (j + 1) * chunk)
        out = jnp.dot(v_cols[...], probs[:, qs], preferred_element_type=F32).astype(BF16)
        grad = jnp.dot(k_cols[...], dscores[:, qs], preferred_element_type=F32) * SCALE
        grad = grad.astype(BF16)
        for i in range(chunk // tokens):
            r = j * (chunk // tokens) + i
            att[:, r * d : (r + 1) * d] = out[:, i * tokens : (i + 1) * tokens].T
            dq[:, r * d : (r + 1) * d] = grad[:, i * tokens : (i + 1) * tokens].T
    for copy in list(y_copies.values()) + list(c_copies.values()):
        copy.wait_send()
    rows = slice(0, back_slots * 2 * piece)
    total = together(*own_grads, F32)[rows]
    for role in (CROSS, FAR, NEAR):
        b_copies[role].wait_recv()
        total += back[role, rows].astype(F32)
    grad_stage[rows] = total.astype(BF16)
    z_copies = {}
    for slot in reversed(range(1, back_slots)):
        z_copies[slot] = send(
            grad_stage.at[slot_rows(slot)],
            grad_in.at[slot],
            z_send.at[slot],
            z_recv.at[slot],
            (c, lax.rem(h + steps[slot], n_head)),
        )

    def finish(slot, both):
        owner = lax.rem(h + n_head - steps[slot], n_head)
        cols = pl.ds(pl.multiple_of(owner * d, d), d)
        dk_out[:, cols] = both[:piece]
        dv_out[:, cols] = both[piece:]

    finish(0, grad_stage[slot_rows(0)])
    for copy in b_copies.values():
        copy.wait_send()
    for slot in range(back_slots, n_head):
        total = 0.0
        for role in (OWN, CROSS, FAR, NEAR):
            f_copies[role, slot].wait_recv()
            total += far_in[role, slot].astype(F32)
        finish(slot, total.astype(BF16))
    for slot in range(1, back_slots):
        z_copies[slot].wait_recv()
        finish(slot, grad_in[slot])

    for copy in list(f_copies.values()) + list(z_copies.values()):
        copy.wait_send()


def write_out(*refs):
    for i in range(4):
        refs[4 + i][...] = refs[i][...]


def per_device(n_ctx, n_head, queries, keys, values, output_gradient, doc_lengths):
    tokens = queries.shape[0]
    piece = keys.shape[0]
    d = HEAD_SIZE
    heads = queries.shape[1] // d
    width = heads * tokens
    docs = doc_lengths.shape[0]
    hbm_spec = pl.BlockSpec(memory_space=pltpu.HBM)
    vmem_spec = pl.BlockSpec(memory_space=pltpu.VMEM)
    block = (2 * tokens, d)
    dma = pltpu.SemaphoreType.DMA
    results = pl.pallas_call(
        functools.partial(kernel, n_ctx, n_head, tokens, heads),
        out_shape=(
            jax.ShapeDtypeStruct(queries.shape, BF16),
            jax.ShapeDtypeStruct(queries.shape, BF16),
            jax.ShapeDtypeStruct(keys.shape, BF16),
            jax.ShapeDtypeStruct(values.shape, BF16),
        ),
        in_specs=[hbm_spec] * 5,
        out_specs=(vmem_spec,) * 4,
        scratch_shapes=[
            pltpu.VMEM(keys.shape, BF16),
            pltpu.VMEM(values.shape, BF16),
            pltpu.VMEM((1, docs), jnp.int32),
            pltpu.VMEM((tokens, width), BF16),
            pltpu.VMEM((tokens, width), BF16),
            pltpu.VMEM((d, width), BF16),
            pltpu.VMEM((d, width), BF16),
            pltpu.VMEM((n_head, 2 * piece, d), BF16),
            pltpu.VMEM((ROLES, *block), BF16),
            pltpu.VMEM((d, ROLES * tokens), BF16),
            pltpu.VMEM((d, ROLES * tokens), BF16),
            pltpu.VMEM((ROLES * tokens, width), BF16),
            pltpu.VMEM((ROLES * tokens, width), F32),
            pltpu.VMEM((ROLES * tokens, width), BF16),
            pltpu.VMEM((ROLES, *block), BF16),
            pltpu.VMEM((ROLES, *block), BF16),
            pltpu.VMEM(block, BF16),
            pltpu.VMEM((n_head, 2 * piece, d), BF16),
            pltpu.VMEM((4, n_head, 2 * piece, d), BF16),
            dma((5,)),
            dma((n_head,)),
            dma((n_head,)),
            dma((ROLES, 2)),
            dma((ROLES, 2)),
            dma((ROLES,)),
            dma((ROLES,)),
            dma((n_head,)),
            dma((n_head,)),
            dma((4, n_head)),
            dma((4, n_head)),
            pltpu.SemaphoreType.REGULAR,
        ],
        compiler_params=pltpu.CompilerParams(
            collective_id=0, has_side_effects=True, vmem_limit_bytes=40 * 1024 * 1024
        ),
    )(*(
        pltpu.with_memory_space_constraint(x, pltpu.HBM)
        for x in (queries, keys, values, output_gradient, doc_lengths.reshape(1, docs))
    ))
    return pl.pallas_call(
        write_out,
        out_shape=tuple(jax.ShapeDtypeStruct(x.shape, x.dtype) for x in results),
        in_specs=[vmem_spec] * 4,
        out_specs=(vmem_spec,) * 4,
        scratch_shapes=[dma((4,))],
        compiler_params=pltpu.CompilerParams(vmem_limit_bytes=8 * 1024 * 1024),
    )(*results)


def solution(mesh):
    n_ctx, n_head = mesh.shape["ctx"], mesh.shape["head"]
    return jax.shard_map(
        functools.partial(per_device, n_ctx, n_head),
        mesh=mesh,
        in_specs=(
            P("ctx", "head"),
            P(("ctx", "head"), None),
            P(("ctx", "head"), None),
            P("ctx", "head"),
            P(),
        ),
        out_specs=(
            P("ctx", "head"),
            P("ctx", "head"),
            P(("ctx", "head"), None),
            P(("ctx", "head"), None),
        ),
        check_vma=False,
    )
```

```python
import functools

import jax
import jax.numpy as jnp
from jax import lax
from jax.experimental import pallas as pl
from jax.experimental.pallas import tpu as pltpu
from jax.sharding import PartitionSpec as P

HEAD_SIZE = 128
SCALE = HEAD_SIZE ** (-0.5)
LOG2E = 1.4426950408889634
big_negative = -1e30
MESH = pl.DeviceIdType.MESH
F32 = jnp.float32
BF16 = jnp.bfloat16

OWN = 0
NEAR = 1
FAR = 2
CROSS = 3
NEAR_SIB = 4
FAR_SIB = 5
ROLES = 6


def ring_steps(n):
    return sorted(range(n), key=lambda step: (min(step, n - step), step))


class Message:
    def __init__(self, src, dst, send_sem, recv_sem, to, sends=None, receives=None):
        self.copy = pltpu.make_async_remote_copy(
            src_ref=src,
            dst_ref=dst,
            send_sem=send_sem,
            recv_sem=recv_sem,
            device_id=to,
            device_id_type=MESH,
        )
        self.sends, self.receives = sends, receives

    def start(self):
        run_if(self.sends, self.copy.start)

    def wait_recv(self):
        run_if(self.receives, self.copy.wait_recv)

    def wait_send(self):
        run_if(self.sends, self.copy.wait_send)


def run_if(condition, action):
    if condition is None:
        action()
        return

    @pl.when(condition)
    def _():
        action()


def kernel(
    n_ctx,
    n_head,
    tokens,
    heads,
    q_hbm,
    k_hbm,
    v_hbm,
    g_hbm,
    len_hbm,
    att,
    dq,
    dk_out,
    dv_out,
    k_in,
    v_in,
    lens,
    q_in,
    g_in,
    q_cols,
    g_cols,
    kv_stage,
    kv,
    k_cols,
    v_cols,
    probs,
    dprobs,
    dscores,
    part,
    back,
    grad_stage,
    grad_in,
    far_in,
    in_sem,
    y_send,
    y_recv,
    c_send,
    c_recv,
    b_send,
    b_recv,
    z_send,
    z_recv,
    f_send,
    f_recv,
    ready,
):
    d = HEAD_SIZE
    c = lax.axis_index("ctx")
    h = lax.axis_index("head")
    core = lax.rem(c, 2)
    piece = tokens // n_head
    width = heads * tokens
    steps = ring_steps(n_head)
    near_slots = 3
    back_slots = n_head - 5
    groups = (pl.ds(0, near_slots * 2 * piece), pl.ds(near_slots * 2 * piece, (n_head - near_slots) * 2 * piece))

    def slot_rows(slot):
        return pl.ds(slot * 2 * piece, 2 * piece)

    sibling = c + 1 - 2 * core
    cross_to = c + 1 + 4 * core
    cross_from = c + 4 * core - 5
    has_from = {NEAR: c >= 2, FAR: c >= 4, CROSS: cross_from >= 0}
    has_to = {NEAR: c + 2 < n_ctx, FAR: c + 4 < n_ctx, CROSS: cross_to < n_ctx}

    loads = [
        pltpu.make_async_copy(source, target, in_sem.at[i])
        for i, (source, target) in enumerate(
            ((k_hbm, k_in), (v_hbm, v_in), (len_hbm, lens), (q_hbm, q_in), (g_hbm, g_in))
        )
    ]
    barrier = pltpu.get_barrier_semaphore()

    def greet(peer):
        pl.semaphore_signal(barrier, inc=1, device_id=peer, device_id_type=MESH)

    for step in reversed(steps[1:]):
        greet((c, lax.rem(h + step, n_head)))
    later = ((has_to[FAR], c + 4), (has_to[CROSS] & (core == 1), cross_to), (has_to[NEAR], c + 2))
    earlier = (
        (has_from[FAR], c - 4),
        (has_from[CROSS] & (core == 0), cross_from),
        (has_from[NEAR], c - 2),
    )
    for there, peer in later:
        run_if(there, functools.partial(greet, (peer, h)))
    greet((sibling, h))
    n_later = sum(jnp.where(there, 1, 0) for there, _ in later)
    n_earlier = sum(jnp.where(there, 1, 0) for there, _ in earlier)

    loads[0].start()
    loads[1].start()
    for load in loads[2:]:
        load.start()
    loads[0].wait()
    loads[1].wait()
    for r in range(n_head):
        cols = slice(r * d, (r + 1) * d)
        kv_stage[r, :piece] = k_in[:, cols]
        kv_stage[r, piece:] = v_in[:, cols]
    kv[OWN, slot_rows(0)] = kv_stage[h]
    pl.semaphore_wait(barrier, n_head + n_earlier)

    def send(src, dst, send_sem, recv_sem, to, sends=None, receives=None):
        copy = Message(src, dst, send_sem, recv_sem, to, sends, receives)
        copy.start()
        return copy

    y_copies = {}
    for step in reversed(steps[1:]):
        to, slot = lax.rem(h + step, n_head), steps.index(n_head - step)
        y_copies[slot] = send(
            kv_stage.at[to], kv.at[OWN, slot_rows(slot)], y_send.at[slot], y_recv.at[slot], (c, to)
        )

    def tell(peer):
        pl.semaphore_signal(ready, inc=1, device_id=(peer, h), device_id_type=MESH)

    for there, peer in earlier:
        run_if(there, functools.partial(tell, peer))

    for role in (NEAR, FAR, CROSS):

        @pl.when(jnp.logical_not(has_from[role]))
        def _(role=role):
            kv[role] = jnp.zeros(kv.shape[1:], BF16)

        @pl.when(jnp.logical_not(has_to[role]))
        def _(role=role):
            back[role] = jnp.zeros(back.shape[1:], BF16)
            far_in[role] = jnp.zeros(far_in.shape[1:], BF16)

    loads[2].wait()
    ids_row = lax.broadcasted_iota(jnp.int32, (128, 128), 0)
    ids_col = lax.broadcasted_iota(jnp.int32, (128, 128), 1)
    ends = jnp.sum(
        jnp.where(ids_col <= ids_row, jnp.broadcast_to(lens[...], (128, 128)), 0).astype(F32),
        axis=1,
        keepdims=True,
    ).astype(jnp.int32)
    place = c * tokens + ids_col
    starts = jnp.max(jnp.where(ends <= place, ends, 0).astype(F32), axis=0, keepdims=True)
    starts = starts.astype(jnp.int32) - c * tokens
    starts = jnp.concatenate([starts] * 2, axis=1)

    c_copies = {}

    def send_on(source, role, to, group):
        rows = groups[group]
        c_copies[role, group] = send(
            kv.at[source, rows],
            kv.at[role, rows],
            c_send.at[role, group],
            c_recv.at[role, group],
            (to, h),
            has_to.get(role),
            has_from.get(role),
        )

    for group, slots in enumerate((range(1, near_slots), range(near_slots, n_head))):
        for slot in slots:
            y_copies[slot].wait_recv()
        if group == 0:
            run_if(n_later > 0, lambda: pl.semaphore_wait(ready, n_later))
        for role, to in ((FAR, c + 4), (CROSS, cross_to), (NEAR, c + 2)):
            send_on(OWN, role, to, group)

    loads[3].wait()
    loads[4].wait()
    for r in range(heads):
        cols = slice(r * d, (r + 1) * d)
        q_cols[:, cols] = q_in[:, cols].T
        g_cols[:, cols] = g_in[:, cols].T

    chunk = 2 * tokens
    chunks = width // chunk
    key_rows = lax.broadcasted_iota(jnp.int32, (tokens, chunk), 0)
    key_slots = key_rows // piece
    key_steps = jnp.where(key_slots % 2 == 1, (key_slots + 1) // 2, n_head - key_slots // 2)
    key_ids = lax.rem(h + key_steps, n_head) * piece + lax.rem(key_rows, piece)
    query_ids = lax.rem(lax.broadcasted_iota(jnp.int32, (tokens, chunk), 1), tokens)
    back_by = [0, 2, 4, 5 - 4 * core, 1 + 2 * core, 3 + 2 * core]
    tops, totals, deltas = {}, {}, {}

    def apart(both):
        both = both.reshape(n_head, 2, piece, d)
        return both[:, 0].reshape(tokens, d), both[:, 1].reshape(tokens, d)

    def forward(*roles):
        first, count = min(roles), len(roles)
        blocks = [apart(kv[role]) for role in range(first, first + count)]
        k_block = jnp.concatenate([block[0] for block in blocks], axis=0)
        v_block = jnp.concatenate([block[1] for block in blocks], axis=0)
        rows = slice(first * tokens, (first + count) * tokens)
        k_cols[:, rows] = k_block.T
        v_cols[:, rows] = v_block.T
        for j in range(chunks):
            qs = slice(j * chunk, (j + 1) * chunk)
            all_scores = jnp.dot(k_block, q_cols[:, qs], preferred_element_type=F32)
            all_dp = jnp.dot(v_block, g_cols[:, qs], preferred_element_type=F32)
            for i in range(count):
                role = first + i
                part_rows = slice(i * tokens, (i + 1) * tokens)
                visible = key_ids - back_by[role] * tokens >= starts
                if role == OWN:
                    visible = visible & (key_ids <= query_ids)
                scores = jnp.where(visible, all_scores[part_rows], big_negative)
                top = jnp.max(scores, axis=0, keepdims=True)
                grown = jnp.exp2((scores - top) * (SCALE * LOG2E))
                dp = all_dp[part_rows]
                tops[role, j] = top
                totals[role, j] = jnp.sum(grown, axis=0, keepdims=True)
                deltas[role, j] = jnp.sum(grown * dp, axis=0, keepdims=True)
                cols = slice(role * tokens, (role + 1) * tokens)
                probs[cols, qs] = grown.astype(BF16)
                dprobs[cols, qs] = dp

    forward(OWN)
    for role, there in ((NEAR, NEAR_SIB), (FAR, FAR_SIB)):
        for group in range(2):
            c_copies[role, group].wait_recv()
        c_copies[there] = send(
            kv.at[role], kv.at[there], c_send.at[there, 0], c_recv.at[there, 0], (sibling, h)
        )
        if role == NEAR:
            forward(NEAR)
    for group in range(2):
        c_copies[CROSS, group].wait_recv()
    forward(FAR, CROSS)
    for role in (NEAR_SIB, FAR_SIB):
        c_copies[role].wait_recv()
    forward(NEAR_SIB, FAR_SIB)

    factors, delta = {}, {}
    for j in range(chunks):
        top = functools.reduce(jnp.maximum, [tops[role, j] for role in range(ROLES)])
        lift = [jnp.exp2((tops[role, j] - top) * (SCALE * LOG2E)) for role in range(ROLES)]
        total = sum(lift[role] * totals[role, j] for role in range(ROLES))
        for role in range(ROLES):
            factors[role, j] = lift[role] / total
        delta[j] = sum(factors[role, j] * deltas[role, j] for role in range(ROLES))

    def backward(*roles):
        first, count = min(roles), len(roles)
        dk_part = dv_part = 0.0
        for j in range(chunks):
            qs = slice(j * chunk, (j + 1) * chunk)
            ps, dss = [], []
            for role in range(first, first + count):
                rows = slice(role * tokens, (role + 1) * tokens)
                p = probs[rows, qs].astype(F32) * factors[role, j]
                ds = (p * (dprobs[rows, qs] - delta[j])).astype(BF16)
                p = p.astype(BF16)
                probs[rows, qs] = p
                dscores[rows, qs] = ds
                ps.append(p)
                dss.append(ds)
            dk_part += jnp.dot(
                jnp.concatenate(dss, axis=0), by_rows(q_in, j), preferred_element_type=F32
            )
            dv_part += jnp.dot(
                jnp.concatenate(ps, axis=0), by_rows(g_in, j), preferred_element_type=F32
            )
        cut = [slice(i * tokens, (i + 1) * tokens) for i in range(count)]
        return {first + i: (dk_part[cut[i]] * SCALE, dv_part[cut[i]]) for i in range(count)}

    def by_rows(ref, j):
        pair = [
            ref[:, r * d : (r + 1) * d]
            for r in range(j * chunk // tokens, (j + 1) * chunk // tokens)
        ]
        return jnp.concatenate(pair, axis=0)

    def together(dk_part, dv_part, dtype):
        pieces = [x.astype(dtype).reshape(n_head, 1, piece, d) for x in (dk_part, dv_part)]
        return jnp.concatenate(pieces, axis=1).reshape(2 * tokens, d)

    def put(where, dk_part, dv_part):
        where[...] = together(dk_part, dv_part, BF16)

    def with_back(role, dk_part, dv_part):
        b_copies[role].wait_recv()
        dk_back, dv_back = apart(back[role])
        return dk_part + dk_back.astype(F32), dv_part + dv_back.astype(F32)

    b_copies, f_copies = {}, {}

    def send_back(role, to, rows):
        b_copies[role] = send(
            part.at[role, rows],
            back.at[role, rows],
            b_send.at[role],
            b_recv.at[role],
            (to, h),
            has_from.get(role),
            has_to.get(role),
        )

    def send_far(role, to):
        for slot in reversed(range(back_slots, n_head)):
            f_copies[role, slot] = send(
                part.at[role, slot_rows(slot)],
                far_in.at[role, slot],
                f_send.at[role, slot],
                f_recv.at[role, slot],
                (to, lax.rem(h + steps[slot], n_head)),
                has_from.get(role),
                has_to.get(role),
            )

    whole = pl.ds(0, 2 * tokens)
    grads = backward(NEAR_SIB, FAR_SIB)
    for role in (FAR_SIB, NEAR_SIB):
        put(part.at[role], *grads[role])
        send_back(role, sibling, whole)
    grads = backward(FAR, CROSS)
    put(part.at[CROSS], *grads[CROSS])
    send_far(CROSS, cross_from)
    send_back(CROSS, cross_from, pl.ds(0, back_slots * 2 * piece))
    put(part.at[FAR], *with_back(FAR_SIB, *grads[FAR]))
    send_far(FAR, c - 4)
    send_back(FAR, c - 4, pl.ds(0, back_slots * 2 * piece))
    grads = backward(OWN, NEAR)
    put(part.at[NEAR], *with_back(NEAR_SIB, *grads[NEAR]))
    send_far(NEAR, c - 2)
    send_back(NEAR, c - 2, pl.ds(0, back_slots * 2 * piece))
    put(part.at[OWN], *grads[OWN])
    send_far(OWN, c)
    own_grads = grads[OWN]

    for j in range(chunks):
        qs = slice(j * chunk, (j + 1) * chunk)
        out = jnp.dot(v_cols[...], probs[:, qs], preferred_element_type=F32).astype(BF16)
        grad = jnp.dot(k_cols[...], dscores[:, qs], preferred_element_type=F32) * SCALE
        grad = grad.astype(BF16)
        for i in range(chunk // tokens):
            r = j * (chunk // tokens) + i
            att[:, r * d : (r + 1) * d] = out[:, i * tokens : (i + 1) * tokens].T
            dq[:, r * d : (r + 1) * d] = grad[:, i * tokens : (i + 1) * tokens].T
    for copy in list(y_copies.values()) + list(c_copies.values()):
        copy.wait_send()
    rows = slice(0, back_slots * 2 * piece)
    total = together(*own_grads, F32)[rows]
    for role in (CROSS, FAR, NEAR):
        b_copies[role].wait_recv()
        total += back[role, rows].astype(F32)
    grad_stage[rows] = total.astype(BF16)
    z_copies = {}
    for slot in reversed(range(1, back_slots)):
        z_copies[slot] = send(
            grad_stage.at[slot_rows(slot)],
            grad_in.at[slot],
            z_send.at[slot],
            z_recv.at[slot],
            (c, lax.rem(h + steps[slot], n_head)),
        )

    def finish(slot, both):
        owner = lax.rem(h + n_head - steps[slot], n_head)
        cols = pl.ds(pl.multiple_of(owner * d, d), d)
        dk_out[:, cols] = both[:piece]
        dv_out[:, cols] = both[piece:]

    finish(0, grad_stage[slot_rows(0)])
    for copy in b_copies.values():
        copy.wait_send()
    for slot in range(back_slots, n_head):
        total = 0.0
        for role in (OWN, CROSS, FAR, NEAR):
            f_copies[role, slot].wait_recv()
            total += far_in[role, slot].astype(F32)
        finish(slot, total.astype(BF16))
    for slot in range(1, back_slots):
        z_copies[slot].wait_recv()
        finish(slot, grad_in[slot])

    for copy in list(f_copies.values()) + list(z_copies.values()):
        copy.wait_send()


def write_out(*refs):
    for i in range(4):
        refs[4 + i][...] = refs[i][...]


def per_device(n_ctx, n_head, queries, keys, values, output_gradient, doc_lengths):
    tokens = queries.shape[0]
    piece = keys.shape[0]
    d = HEAD_SIZE
    heads = queries.shape[1] // d
    width = heads * tokens
    docs = doc_lengths.shape[0]
    hbm_spec = pl.BlockSpec(memory_space=pltpu.HBM)
    vmem_spec = pl.BlockSpec(memory_space=pltpu.VMEM)
    block = (2 * tokens, d)
    dma = pltpu.SemaphoreType.DMA
    results = pl.pallas_call(
        functools.partial(kernel, n_ctx, n_head, tokens, heads),
        out_shape=(
            jax.ShapeDtypeStruct(queries.shape, BF16),
            jax.ShapeDtypeStruct(queries.shape, BF16),
            jax.ShapeDtypeStruct(keys.shape, BF16),
            jax.ShapeDtypeStruct(values.shape, BF16),
        ),
        in_specs=[hbm_spec] * 5,
        out_specs=(vmem_spec,) * 4,
        scratch_shapes=[
            pltpu.VMEM(keys.shape, BF16),
            pltpu.VMEM(values.shape, BF16),
            pltpu.VMEM((1, docs), jnp.int32),
            pltpu.VMEM((tokens, width), BF16),
            pltpu.VMEM((tokens, width), BF16),
            pltpu.VMEM((d, width), BF16),
            pltpu.VMEM((d, width), BF16),
            pltpu.VMEM((n_head, 2 * piece, d), BF16),
            pltpu.VMEM((ROLES, *block), BF16),
            pltpu.VMEM((d, ROLES * tokens), BF16),
            pltpu.VMEM((d, ROLES * tokens), BF16),
            pltpu.VMEM((ROLES * tokens, width), BF16),
            pltpu.VMEM((ROLES * tokens, width), F32),
            pltpu.VMEM((ROLES * tokens, width), BF16),
            pltpu.VMEM((ROLES, *block), BF16),
            pltpu.VMEM((ROLES, *block), BF16),
            pltpu.VMEM(block, BF16),
            pltpu.VMEM((n_head, 2 * piece, d), BF16),
            pltpu.VMEM((4, n_head, 2 * piece, d), BF16),
            dma((5,)),
            dma((n_head,)),
            dma((n_head,)),
            dma((ROLES, 2)),
            dma((ROLES, 2)),
            dma((ROLES,)),
            dma((ROLES,)),
            dma((n_head,)),
            dma((n_head,)),
            dma((4, n_head)),
            dma((4, n_head)),
            pltpu.SemaphoreType.REGULAR,
        ],
        compiler_params=pltpu.CompilerParams(
            collective_id=0, has_side_effects=True, vmem_limit_bytes=40 * 1024 * 1024
        ),
    )(*(
        pltpu.with_memory_space_constraint(x, pltpu.HBM)
        for x in (queries, keys, values, output_gradient, doc_lengths.reshape(1, docs))
    ))
    return pl.pallas_call(
        write_out,
        out_shape=tuple(jax.ShapeDtypeStruct(x.shape, x.dtype) for x in results),
        in_specs=[vmem_spec] * 4,
        out_specs=(vmem_spec,) * 4,
        scratch_shapes=[dma((4,))],
        compiler_params=pltpu.CompilerParams(vmem_limit_bytes=8 * 1024 * 1024),
    )(*results)


def solution(mesh):
    n_ctx, n_head = mesh.shape["ctx"], mesh.shape["head"]
    return jax.shard_map(
        functools.partial(per_device, n_ctx, n_head),
        mesh=mesh,
        in_specs=(
            P("ctx", "head"),
            P(("ctx", "head"), None),
            P(("ctx", "head"), None),
            P("ctx", "head"),
            P(),
        ),
        out_specs=(
            P("ctx", "head"),
            P("ctx", "head"),
            P(("ctx", "head"), None),
            P(("ctx", "head"), None),
        ),
        check_vma=False,
    )
```
